128 devices in a mesh: sx: 4 (over y), sy: 4 (over x), gz: 8 (over z, core).
Axes of the slice: x: 4, y: 4, z: 4, core: 2. Of those that a mesh axis runs over, the one named last changes fastest.
Arguments:
- observed: float32 [512, 64, 512], P('gz', 'sx', 'sy'), may hold values from 0.25 to 2
- zone_of_slice: int32 [512], P('gz'), may hold values from 0 to 7
- lateral_x: float32 [8, 7], replicated, may hold values from 0.05 to 1
- lateral_y: float32 [8, 7], replicated, may hold values from 0.05 to 1
- depth_psf: float32 [17], replicated, may hold values from 0.05 to 1
- stitch_width: int32 [4, 4, 2], replicated, may hold values from 1 to 8
Outputs:
- estimate: float32 [512, 64, 512], P('gz', 'sx', 'sy')
The draws below stay inside these ranges and needn't reach their ends.
All inputs are finite; a program needn't handle non-finite values.
Results may differ from the reference program's by a relative error of at most 0.0001.
Values sent between devices are 32-bit elements; how exact they have to be, the bound alone decides.
A program may use at most 64 MiB of HBM per device.

```python
import math
import jax
import jax.numpy as jnp
from jax import lax

NZ = 512
CX = 16
CY = 128
ZONES = 8
ITERS = 2
TAPS = 7
DEPTH_TAPS = 17
NX = 64
NY = 512
STACKS_X = 4
STACKS_Y = 4


def set_ends(values, key, least, top_value):
    spot = [jax.random.randint(jax.random.fold_in(key, axis), (), 0, length) for axis, length in enumerate(values.shape)]
    longest = values.shape.index(max(values.shape))
    beside = spot[:longest] + [(spot[longest] + 1) % values.shape[longest]] + spot[longest + 1:]
    return values.at[tuple(spot)].set(least).at[tuple(beside)].set(top_value)


def block_scale(rng, dims, split, least, high):
    factor_of, own = 1.0, jax.random.fold_in(rng, 6)
    for axis_at, shards_of in split:
        draws = jnp.exp(jax.random.uniform(jax.random.fold_in(own, axis_at), (shards_of,), jnp.float32, least / len(split), high / len(split)))
        factor_of = factor_of * jnp.repeat(draws, dims[axis_at] // shards_of).reshape([-1 if axis == axis_at else 1 for axis in range(len(dims))])
    return factor_of


def setup_inputs(seed: int = 0) -> dict:
    key_list = jax.random.split(jax.random.key(seed), 7)
    return {
        "observed": jnp.clip(0.25 + 1.75 * jax.random.uniform(key_list[0], (NZ, NX, NY), jnp.float32) ** block_scale(key_list[0], (NZ, NX, NY), ((0, 8), (1, 4), (2, 4)), -0.2, 0.2), 0.25, 2.0),
        "zone_of_slice": set_ends(jax.random.randint(key_list[1], (NZ,), 0, ZONES), jax.random.fold_in(key_list[1], 1), 0, ZONES - 1).astype(jnp.int32),
        "lateral_x": jnp.clip(jnp.exp(jax.random.uniform(key_list[2], (ZONES, TAPS), jnp.float32, math.log(0.05), math.log(1.0))), 0.05, 1.0),
        "lateral_y": jnp.clip(jnp.exp(jax.random.uniform(key_list[3], (ZONES, TAPS), jnp.float32, math.log(0.05), math.log(1.0))), 0.05, 1.0),
        "depth_psf": jnp.clip(jnp.exp(jax.random.uniform(key_list[4], (DEPTH_TAPS,), jnp.float32, math.log(0.05), math.log(1.0))), 0.05, 1.0),
        "stitch_width": set_ends(jax.random.randint(key_list[5], (STACKS_X, STACKS_Y, 2), 1, CX // 2 + 1), jax.random.fold_in(key_list[5], 1), 1, (CX // 2 + 1) - 1).astype(jnp.int32),
    }


def slice_taps(zone_of_slice, kernels):
    ids = jnp.arange(kernels.shape[0], dtype=jnp.int32)
    onehot = (zone_of_slice[:, None] == ids[None, :]).astype(jnp.float32)
    return jnp.sum(onehot[:, :, None] * kernels[None, :, :], axis=1)


def lateral_core(padded, taps_x, taps_y, width_x, width_y):
    count = taps_x.shape[1]
    along = taps_x[:, 0, None, None] * padded[:, 0:width_x, :]
    for a in range(1, count):
        along = along + taps_x[:, a, None, None] * padded[:, a:a + width_x, :]
    result = taps_y[:, 0, None, None] * along[:, :, 0:width_y]
    for b in range(1, count):
        result = result + taps_y[:, b, None, None] * along[:, :, b:b + width_y]
    return result


def lateral_full(volume, taps_x, taps_y, flip):
    if flip:
        taps_x = taps_x[:, ::-1]
        taps_y = taps_y[:, ::-1]
    reach = (taps_x.shape[1] - 1) // 2
    padded = jnp.pad(volume, ((0, 0), (reach, reach), (reach, reach)))
    return lateral_core(padded, taps_x, taps_y, volume.shape[1], volume.shape[2])


def depth_tables(depth_psf, length):
    kernel = depth_psf / jnp.sum(depth_psf)
    reach = (depth_psf.shape[0] - 1) // 2
    freq = jnp.arange(length, dtype=jnp.int32)
    offs = jnp.arange(depth_psf.shape[0], dtype=jnp.int32) - reach
    phase = jnp.mod(freq[:, None] * offs[None, :], length).astype(jnp.float32) * (2.0 * math.pi / length)
    gain_c = jnp.sum(kernel[None, :] * jnp.cos(phase), axis=1)
    gain_s = jnp.sum(kernel[None, :] * jnp.sin(phase), axis=1)
    pos = jnp.arange(length, dtype=jnp.int32)
    angle = jnp.mod(freq[:, None] * pos[None, :], length).astype(jnp.float32) * (2.0 * math.pi / length)
    table = jnp.concatenate([jnp.cos(angle), jnp.sin(angle)], axis=0)
    return table, gain_c, gain_s


def depth_columns(columns, table, gain_c, gain_s, sign):
    length = table.shape[1]
    coef = jnp.dot(table, columns, precision=lax.Precision.HIGHEST, preferred_element_type=jnp.float32)
    cpart = coef[:length]
    spart = coef[length:]
    upper = cpart * gain_c[:, None] - sign * spart * gain_s[:, None]
    lower = sign * cpart * gain_s[:, None] + spart * gain_c[:, None]
    stacked = jnp.concatenate([upper, lower], axis=0)
    back = lax.dot_general(table, stacked, (((0,), (0,)), ((), ())), precision=lax.Precision.HIGHEST, preferred_element_type=jnp.float32)
    return back / length


def depth_full(volume, table, gain_c, gain_s, sign):
    shape = volume.shape
    flat = volume.reshape(shape[0], -1)
    return depth_columns(flat, table, gain_c, gain_s, sign).reshape(shape)


def reference(observed, zone_of_slice, lateral_x, lateral_y, depth_psf, stitch_width):
    taps_x = slice_taps(zone_of_slice, lateral_x)
    taps_y = slice_taps(zone_of_slice, lateral_y)
    table, gain_c, gain_s = depth_tables(depth_psf, NZ)
    xpos = jnp.arange(NX, dtype=jnp.int32)
    ypos = jnp.arange(NY, dtype=jnp.int32)
    stack_x = xpos // CX
    stack_y = ypos // CY
    band_x = stitch_width[stack_x[:, None], stack_y[None, :], 0]
    band_y = stitch_width[stack_x[:, None], stack_y[None, :], 1]
    weight = jnp.where((xpos % CX)[:, None] < band_x, 0.5, 1.0) * jnp.where((ypos % CY)[None, :] < band_y, 0.5, 1.0)
    weight = weight.astype(jnp.float32)
    weight_vol = jnp.broadcast_to(weight[None, :, :], observed.shape)
    data = weight_vol * observed
    norm = lateral_full(weight_vol, taps_x, taps_y, True)
    estimate = observed
    for step in range(ITERS):
        blurred = depth_full(lateral_full(estimate, taps_x, taps_y, False), table, gain_c, gain_s, 1.0)
        ratio = data / blurred
        update = lateral_full(depth_full(ratio, table, gain_c, gain_s, -1.0), taps_x, taps_y, True)
        estimate = estimate * update / norm
    return estimate
```

```python
import itertools
import jax
import jax.numpy as jnp
from jax import lax
from jax.experimental import pallas as pl
from jax.experimental.pallas import tpu as pltpu
from jax.sharding import PartitionSpec as P

MESH = pl.DeviceIdType.MESH
F32 = jnp.float32
BF16 = jnp.bfloat16
NX, NY, NZ = 16, 128, 64
R = 3
HZ = 16
EZ = NZ + 2 * HZ
EX = NX + 2 * R
SX, SY, GZ = 4, 4, 8
DIRS = [d for d in itertools.product((-1, 0, 1), repeat=3) if d != (0, 0, 0)]
SDIRS = [d for d in DIRS if d[2] == 0]
KX, KY, KYM, KYF = 0, 7, 14, 21


def kernel(
    obs, zone, lat_x, lat_y, psf, stitch, out,
    est1, est2, spr1, spr2, pk, ye1, ye2, ys1, ys2, lest, rnorm, res,
    ktab, taps, tb, in_sem, out_sem, t_sem,
    es1, er1, es2, er2, ss1, sr1, ss2, sr2,
):
    sx, sy, gz = lax.axis_index("sx"), lax.axis_index("sy"), lax.axis_index("gz")
    lane = lax.broadcasted_iota(jnp.int32, (8, 128), 1)
    lane6 = lane % 6
    edge = jnp.logical_or(lane < R, lane >= NY - R)

    loads = [pltpu.make_async_copy(obs.at[:, x, :], est1.at[R + x, pl.ds(HZ, NZ)], in_sem.at[x]) for x in range(NX)]
    for c in loads:
        c.start()

    def inside(dx, dy):
        ok = None
        for at, d, n in ((sx, dx, SX), (sy, dy, SY)):
            if d:
                t = at < n - 1 if d > 0 else at > 0
                ok = t if ok is None else jnp.logical_and(ok, t)
        return ok

    def guarded(cond, fn):
        if cond is None:
            fn()
        else:
            pl.when(cond)(fn)

    def device(dx, dy, dz):
        return (sx + dx, sy + dy, lax.rem(gz + dz + GZ, GZ))

    for dx, slot, rows in ((1, 0, 0), (-1, 2, EX - R)):
        @pl.when(jnp.logical_not(inside(-dx, 0)))
        def _(slot=slot, rows=rows):
            for e in (est1, est2, spr1, spr2):
                e[pl.ds(rows, R)] = jnp.zeros((R,) + e.shape[1:], F32)
            for y in (ye1, ye2, ys1, ys2):
                for side in range(2):
                    y[side, slot] = jnp.zeros(y.shape[2:], F32)
    for dy, side in ((1, 0), (-1, 1)):
        @pl.when(jnp.logical_not(inside(0, -dy)))
        def _(side=side):
            for y in (ye1, ye2, ys1, ys2):
                y[side] = jnp.zeros(y.shape[1:], F32)

    barrier = pltpu.get_barrier_semaphore()
    for dx, dy in itertools.product((-1, 0, 1), repeat=2):
        def greet(dx=dx, dy=dy):
            for dz in (-1, 0, 1):
                if (dx, dy, dz) != (0, 0, 0):
                    pl.semaphore_signal(barrier, inc=1, device_id=device(dx, dy, dz), device_id_type=MESH)
        guarded(inside(dx, dy), greet)

    ktab[...] = jnp.zeros((8, 128), F32)
    ktab[:, 0:7] = lat_x[...]
    ktab[:, 7:14] = lat_y[...]
    for z in range(NZ):
        taps[HZ + z : HZ + z + 1, :] = ktab[pl.ds(zone[z], 1), :]

    def make_taps(g, _):
        rows = pl.ds(pl.multiple_of(g * 8, 8), 8)
        t = taps[rows, :]
        for i in range(14):
            tb[i, rows, :] = jnp.broadcast_to(t[:, i : i + 1], (8, 128))
        for b in range(7):
            reach = lane + (b - R)
            ok = jnp.logical_and(reach >= 0, reach < NY)
            tb[KYM + b, rows, :] = jnp.where(ok, tb[KY + b, rows, :], 0.0)
            tb[KYF + b, rows, :] = jnp.where(ok, tb[KY + 6 - b, rows, :], 0.0)
        return 0

    lax.fori_loop(2, 10, make_taps, 0)

    def pack(src, off, dst):
        def body(g, _):
            rows = pl.ds(pl.multiple_of(g * 8 + off, 8), 8)
            acc = jnp.zeros((8, 128), F32)
            for x in range(NX):
                v = pltpu.roll(src[R + x, rows, :], 6 * x + R, 1)
                acc = jnp.where(jnp.logical_and(lane >= 6 * x, lane < 6 * x + 6), v, acc)
            dst[pl.ds(pl.multiple_of(g * 8, 8), 8), :] = acc
            return 0

        lax.fori_loop(0, NZ // 8, body, 0)

    def copies(main, strips, packed, halo, dirs, send, recv):
        found = {}
        for i, (dx, dy, dz) in enumerate(dirs):
            zs, zd, n = {0: (0, halo, NZ), 1: (NZ - HZ, 0, HZ), -1: (0, halo + NZ, HZ)}[dz]
            if dy == 0:
                xs, xd, m = {0: (R, R, NX), 1: (NX, 0, R), -1: (R, R + NX, R)}[dx]
                src = main.at[pl.ds(xs, m), pl.ds(halo + zs, n), :]
                dst = main.at[pl.ds(xd, m), pl.ds(zd, n), :]
            else:
                src = packed.at[pl.ds(zs, n), :]
                dst = strips.at[0 if dy > 0 else 1, 1 - dx, pl.ds(zd, n), :]
            found[(dx, dy, dz)] = pltpu.make_async_remote_copy(
                src_ref=src, dst_ref=dst, send_sem=send.at[i], recv_sem=recv.at[i],
                device_id=device(dx, dy, dz), device_id_type=MESH)
        return found

    def each(found, sign, what):
        for dx, dy in sorted({d[:2] for d in found}, key=lambda d: -abs(d[0]) - abs(d[1])):
            def go(dx=dx, dy=dy):
                for d, c in found.items():
                    if d[:2] == (dx, dy):
                        getattr(c, what)()
            guarded(inside(sign * dx, sign * dy), go)

    def lateral(rows_of, strips_of, flip, sink, lo, hi, off):
        def body(g, _):
            trow = pl.ds(pl.multiple_of(g * 8 + off, 8), 8)
            kx = [tb[KX + (6 - a if flip else a), trow, :] for a in range(7)]
            ky = [tb[KY + (6 - b if flip else b), trow, :] for b in range(7)]
            c, cu, cd = strips_of(g)
            cu, cd = pltpu.roll(cu, 32, 1), pltpu.roll(cd, 96, 1)
            c2 = jnp.where(lane < 96, c, cd)
            c1 = jnp.where(lane < 110, c2, cu)
            al = kx[3] * c
            for a in (0, 1, 2, 4, 5, 6):
                al = al + kx[a] * pltpu.roll(c2 if a == 6 else c1, (18 - 6 * a) % 128, 1)
            sc = jnp.zeros((8, 128), F32)
            for b in (0, 1, 2, 4, 5, 6):
                ok = {0: lane6 >= 3, 1: jnp.logical_or(lane6 == 3, lane6 == 4), 2: lane6 == 3,
                      4: lane6 == 2, 5: jnp.logical_or(lane6 == 1, lane6 == 2), 6: lane6 <= 2}[b]
                sc = sc + jnp.where(ok, ky[b] * pltpu.roll(al, (R - b) % 128, 1), 0.0)
            kym = [tb[(KYF if flip else KYM) + b, trow, :] for b in range(7)]
            window = [rows_of(x, g) for x in range(6)]
            for x in range(NX):
                window.append(rows_of(x + 6, g))
                along = kx[0] * window[0]
                for a in range(1, 7):
                    along = along + kx[a] * window[a]
                window = window[1:]
                acc = kym[3] * along
                for b in (0, 1, 2, 4, 5, 6):
                    acc = acc + kym[b] * pltpu.roll(along, (R - b) % 128, 1)
                acc = acc + jnp.where(edge, pltpu.roll(sc, (-(6 * x + R)) % 128, 1), 0.0)
                sink(x, g, acc)
            return 0

        lax.fori_loop(lo, hi, body, 0)

    def rows_from(ref):
        return lambda x, g: ref[x, pl.ds(pl.multiple_of(g * 8, 8), 8), :]

    left = lane6 < R

    def strips_from(ref):
        def get(g):
            r = pl.ds(pl.multiple_of(g * 8, 8), 8)
            return tuple(jnp.where(left, ref[0, s, r, :], ref[1, s, r, :]) for s in (1, 0, 2))
        return get

    def band(i, j, k):
        return stitch[jnp.clip(sx + i, 0, SX - 1), jnp.clip(sy + j, 0, SY - 1), k]

    def half(pos, width):
        return jnp.where(pos < width, 0.5, 1.0).astype(F32)

    wrows = []
    for x in range(-R, NX + R):
        i = -1 if x < 0 else (1 if x >= NX else 0)
        row = half(jnp.full((8, 128), x - i * NX, jnp.int32), band(i, 0, 0)) * half(lane, band(i, 0, 1))
        cond = inside(i, 0)
        if cond is not None:
            row = row * jnp.where(cond, 1.0, 0.0).astype(F32)
        wrows.append(row)
    wstrips = []
    for i in (0, -1, 1):
        parts = []
        for j, pos in ((-1, NY - R + lane6), (1, lane6 - R)):
            v = half(lane // 6, band(i, j, 0)) * half(pos, band(i, j, 1))
            parts.append(v * jnp.where(inside(i, j), 1.0, 0.0).astype(F32))
        wstrips.append(jnp.where(left, parts[0], parts[1]))

    total = psf[0]
    for j in range(1, 17):
        total = total + psf[j]

    def depth_matrix(m, k, forward):
        off = lax.broadcasted_iota(jnp.int32, (m, k), 1) - lax.broadcasted_iota(jnp.int32, (m, k), 0)
        h = jnp.zeros((m, k), F32)
        for j in range(17):
            h = jnp.where(off == j, psf[16 - j if forward else j], h)
        h = h / jnp.full((m, k), total, F32)
        hi = h.astype(BF16)
        lo = (h - hi.astype(F32)).astype(BF16)
        return jnp.concatenate([hi, hi, lo], axis=1)

    def split3(v):
        hi = v.astype(BF16)
        lo = (v - hi.astype(F32)).astype(BF16)
        return hi, lo

    for c in loads:
        c.wait()
    pack(est1, HZ, pk.at[0])
    nx = 3 - (sx == 0).astype(jnp.int32) - (sx == SX - 1).astype(jnp.int32)
    ny = 3 - (sy == 0).astype(jnp.int32) - (sy == SY - 1).astype(jnp.int32)
    pl.semaphore_wait(barrier, nx * ny * 3 - 1)

    tcopies = [
        pltpu.make_async_remote_copy(
            src_ref=taps.at[pl.ds(s, HZ), :], dst_ref=taps.at[pl.ds(d, HZ), :],
            send_sem=t_sem.at[0, i], recv_sem=t_sem.at[1, i], device_id=device(0, 0, dz), device_id_type=MESH)
        for i, (dz, s, d) in enumerate(((1, NZ, 0), (-1, HZ, HZ + NZ)))
    ]
    for c in tcopies:
        c.start()
    e1 = copies(est1, ye1, pk.at[0], HZ, DIRS, es1, er1)
    s1 = copies(spr1, ys1, pk.at[1], 0, SDIRS, ss1, sr1)
    e2 = copies(est2, ye2, pk.at[2], HZ, DIRS, es2, er2)
    s2 = copies(spr2, ys2, pk.at[3], 0, SDIRS, ss2, sr2)
    each(e1, 1, "start")

    def keep_norm(x, g, v):
        rnorm[x, pl.ds(pl.multiple_of(g * 8, 8), 8), :] = 1.0 / v

    lateral(lambda x, g: wrows[x], lambda g: wstrips, True, keep_norm, 0, NZ // 8, HZ)
    for c in tcopies:
        c.wait_recv()
    lax.fori_loop(0, 2, make_taps, 0)
    lax.fori_loop(10, 12, make_taps, 0)

    fwd1 = depth_matrix(48, 64, True)
    fwd2 = depth_matrix(32, 48, True)
    bwd = depth_matrix(64, 80, False)

    def keep_lest(x, g, v):
        lest[x, pl.ds(pl.multiple_of(g * 8, 8), 8), :] = v

    for est, ye, ecop, spr, ys, scop, pks, last in (
        (est1, ye1, e1, spr1, ys1, s1, 1, False),
        (est2, ye2, e2, spr2, ys2, s2, 3, True),
    ):
        each(ecop, -1, "wait_recv")
        lateral(rows_from(est), strips_from(ye), False, keep_lest, 0, EZ // 8, 0)
        for p in (0, 1, 6, 7, 2, 3, 4, 5):
            a, b = 2 * p, 2 * p + 1
            hi, lo = split3(jnp.concatenate([lest[a], lest[b]], axis=1))
            top = jnp.concatenate([hi[0:64], lo[0:64], hi[0:64]], axis=0)
            low = jnp.concatenate([hi[48:96], lo[48:96], hi[48:96]], axis=0)
            blur = jnp.concatenate(
                [jnp.dot(fwd1, top, preferred_element_type=F32), jnp.dot(fwd2, low, preferred_element_type=F32)], axis=0)
            wide = jnp.concatenate([wrows[R + a][0:1], wrows[R + b][0:1]], axis=1)
            seen = jnp.concatenate([est1[R + a, 8:88, :], est1[R + b, 8:88, :]], axis=1)
            hi, lo = split3(wide * seen / blur)
            back = jnp.dot(bwd, jnp.concatenate([hi, lo, hi], axis=0), preferred_element_type=F32)
            spr[R + a] = back[:, 0:128]
            spr[R + b] = back[:, 128:256]
        pack(spr, 0, pk.at[pks])
        each(scop, 1, "start")
        each(scop, -1, "wait_recv")

        def keep_est(x, g, v, est=est, last=last):
            r = pl.ds(pl.multiple_of(g * 8, 8), 8)
            rz = pl.ds(pl.multiple_of(g * 8 + HZ, 8), 8)
            new = est[R + x, rz, :] * v * rnorm[x, r, :]
            if last:
                res[x, r, :] = new
            else:
                est2[R + x, rz, :] = new

        lateral(rows_from(spr), strips_from(ys), True, keep_est, 0, NZ // 8, HZ)
        if not last:
            pack(est2, HZ, pk.at[2])
            each(e2, 1, "start")

    stores = [pltpu.make_async_copy(res.at[x], out.at[:, x, :], out_sem.at[x]) for x in range(NX)]
    for c in stores:
        c.start()
    for c in tcopies:
        c.wait_send()
    for found in (e1, s1, e2, s2):
        each(found, 1, "wait_send")
    for c in stores:
        c.wait()


def body(observed, zone_of_slice, lateral_x, lateral_y, depth_psf, stitch_width):
    any_spec = pl.BlockSpec(memory_space=pl.ANY)
    smem = pl.BlockSpec(memory_space=pltpu.SMEM)
    vmem = pl.BlockSpec(memory_space=pltpu.VMEM)
    dma = pltpu.SemaphoreType.DMA
    ne, ns = len(DIRS), len(SDIRS)
    return pl.pallas_call(
        kernel,
        out_shape=jax.ShapeDtypeStruct(observed.shape, F32),
        in_specs=[any_spec, smem, vmem, vmem, smem, smem],
        out_specs=any_spec,
        scratch_shapes=[
            pltpu.VMEM((EX, EZ, NY), F32), pltpu.VMEM((EX, EZ, NY), F32),
            pltpu.VMEM((EX, NZ, NY), F32), pltpu.VMEM((EX, NZ, NY), F32),
            pltpu.VMEM((4, NZ, 128), F32),
            pltpu.VMEM((2, 3, EZ, 128), F32), pltpu.VMEM((2, 3, EZ, 128), F32),
            pltpu.VMEM((2, 3, NZ, 128), F32), pltpu.VMEM((2, 3, NZ, 128), F32),
            pltpu.VMEM((NX, EZ, NY), F32), pltpu.VMEM((NX, NZ, NY), F32), pltpu.VMEM((NX, NZ, NY), F32),
            pltpu.VMEM((8, 128), F32), pltpu.VMEM((EZ, 128), F32), pltpu.VMEM((28, EZ, 128), F32),
            dma((NX,)), dma((NX,)), dma((2, 2)),
            dma((ne,)), dma((ne,)), dma((ne,)), dma((ne,)),
            dma((ns,)), dma((ns,)), dma((ns,)), dma((ns,)),
        ],
        compiler_params=pltpu.CompilerParams(collective_id=0, has_side_effects=True, vmem_limit_bytes=40 * 1024 * 1024),
        name="deconvolve",
    )(observed, zone_of_slice, lateral_x, lateral_y, depth_psf, stitch_width)


def solution(mesh):
    in_specs = (P("gz", "sx", "sy"), P("gz"), P(), P(), P(), P())
    out_specs = P("gz", "sx", "sy")
    return jax.shard_map(body, mesh=mesh, in_specs=in_specs, out_specs=out_specs, check_vma=False)
```

```python
import itertools
import jax
import jax.numpy as jnp
from jax import lax
from jax.experimental import pallas as pl
from jax.experimental.pallas import tpu as pltpu
from jax.sharding import PartitionSpec as P

MESH = pl.DeviceIdType.MESH
F32 = jnp.float32
BF16 = jnp.bfloat16
NX, NY, NZ = 16, 128, 64
R = 3
HZ = 16
EZ = NZ + 2 * HZ
EX = NX + 2 * R
SX, SY, GZ = 4, 4, 8
DIRS = [d for d in itertools.product((-1, 0, 1), repeat=3) if d != (0, 0, 0)]
SDIRS = [d for d in DIRS if d[2] == 0]
KX, KY = 0, 7
PAIRS = ((0, 1), (2, 4), (5, 6))
CORNERS = {(1, 1): (78, 110), (1, -1): (81, 113), (-1, 1): (0, 96), (-1, -1): (3, 99)}


def kernel(
    obs, zone, lat_x, lat_y, psf, stitch, out,
    est1, est2, spr1, spr2, pk, qk, ye1, ye2, ys1, ys2, qe1, qe2, qs1, qs2, ch, lest, rnorm, res,
    ktab, taps, tb, smat, in_sem, out_sem, t_sem,
    es1, er1, es2, er2, ss1, sr1, ss2, sr2,
):
    sx, sy, gz = lax.axis_index("sx"), lax.axis_index("sy"), lax.axis_index("gz")
    lane = lax.broadcasted_iota(jnp.int32, (8, 128), 1)
    lane6 = lane % 6
    edge = jnp.logical_or(lane < R, lane >= NY - R)

    loads = [pltpu.make_async_copy(obs.at[:, x, :], est1.at[R + x, pl.ds(HZ, NZ)], in_sem.at[x]) for x in range(NX)]
    for c in loads:
        c.start()

    def inside(dx, dy):
        ok = None
        for at, d, n in ((sx, dx, SX), (sy, dy, SY)):
            if d:
                t = at < n - 1 if d > 0 else at > 0
                ok = t if ok is None else jnp.logical_and(ok, t)
        return ok

    def guarded(cond, fn):
        if cond is None:
            fn()
        else:
            pl.when(cond)(fn)

    def device(dx, dy, dz):
        return (sx + dx, sy + dy, lax.rem(gz + dz + GZ, GZ))

    for dx, slot, rows in ((1, 0, 0), (-1, 1, EX - R)):
        @pl.when(jnp.logical_not(inside(-dx, 0)))
        def _(slot=slot, rows=rows):
            for e in (est1, est2, spr1, spr2):
                e[pl.ds(rows, R)] = jnp.zeros((R,) + e.shape[1:], F32)
            for q in (qe1, qe2, qs1, qs2):
                for side in range(2):
                    q[side, slot] = jnp.zeros(q.shape[2:], F32)
    for dy, side in ((1, 0), (-1, 1)):
        @pl.when(jnp.logical_not(inside(0, -dy)))
        def _(side=side):
            for y in (ye1, ye2, ys1, ys2, qe1, qe2, qs1, qs2):
                y[side] = jnp.zeros(y.shape[1:], F32)

    barrier = pltpu.get_barrier_semaphore()
    for dx, dy in itertools.product((-1, 0, 1), repeat=2):
        def greet(dx=dx, dy=dy):
            for dz in (-1, 0, 1):
                if (dx, dy, dz) != (0, 0, 0):
                    pl.semaphore_signal(barrier, inc=1, device_id=device(dx, dy, dz), device_id_type=MESH)
        guarded(inside(dx, dy), greet)

    ktab[...] = jnp.zeros((8, 128), F32)
    ktab[:, 0:7] = lat_x[...]
    ktab[:, 7:14] = lat_y[...]
    for z in range(NZ):
        taps[HZ + z : HZ + z + 1, :] = ktab[pl.ds(zone[z], 1), :]

    def make_taps(g, _):
        rows = pl.ds(pl.multiple_of(g * 8, 8), 8)
        t = taps[rows, :]
        for i in range(14):
            tb[i, rows, :] = jnp.broadcast_to(t[:, i : i + 1], (8, 128))
        return 0


    def place(acc, v, x):
        at = jnp.logical_and(lane >= 6 * x, lane < 6 * x + 6)
        return jnp.where(at, pltpu.roll(v, 6 * x + R, 1), acc)

    def pack_loop(src, off, dst):
        def body(g, _):
            acc = jnp.zeros((8, 128), F32)
            for x in range(NX):
                acc = place(acc, src[R + x, pl.ds(pl.multiple_of(g * 8 + off, 8), 8), :], x)
            dst[pl.ds(pl.multiple_of(g * 8, 8), 8), :] = acc
            return 0

        lax.fori_loop(0, NZ // 8, body, 0)

    def pack_corners(groups, dst):
        for k, (first, _) in enumerate(CORNERS.values()):
            acc = jnp.zeros((8, 128), F32)
            for g in range(NZ // 8):
                at = jnp.logical_and(lane >= 16 * g, lane < 16 * g + 16)
                acc = jnp.where(at, pltpu.roll(groups[g], (16 * g - first) % 128, 1), acc)
            dst[k] = acc

    def unpack_corners(src, halo):
        up = (lane + 4) % 6 < R
        for g in range((NZ + 2 * halo) // 8):
            slot, local = 1, g - halo // 8
            if local < 0:
                slot, local = 0, local + NZ // 8
            elif local >= NZ // 8:
                slot, local = 2, local - NZ // 8
            got = [pltpu.roll(src[0 if d[1] > 0 else 1, 0 if d[0] > 0 else 1, slot], (at - 16 * local) % 128, 1)
                   for d, (_, at) in CORNERS.items()]
            cu = jnp.where(up, got[0], got[1])
            cd = jnp.where(left, got[2], got[3])
            ch[0, g * 8 : g * 8 + 8, :] = jnp.where(lane < 110, cd, cu)
            ch[1, g * 8 : g * 8 + 8, :] = cd

    def copies(main, strips, packed, corners, cpacked, halo, dirs, send, recv):
        found = {}
        for i, (dx, dy, dz) in enumerate(dirs):
            zs, zd, n = {0: (0, halo, NZ), 1: (NZ - HZ, 0, HZ), -1: (0, halo + NZ, HZ)}[dz]
            if dy == 0:
                xs, xd, m = {0: (R, R, NX), 1: (NX, 0, R), -1: (R, R + NX, R)}[dx]
                src = main.at[pl.ds(xs, m), pl.ds(halo + zs, n), :]
                dst = main.at[pl.ds(xd, m), pl.ds(zd, n), :]
            elif dx == 0:
                src = packed.at[pl.ds(zs, n), :]
                dst = strips.at[0 if dy > 0 else 1, pl.ds(zd, n), :]
            else:
                src = cpacked.at[list(CORNERS).index((dx, dy))]
                dst = corners.at[0 if dy > 0 else 1, 0 if dx > 0 else 1, 1 - dz]
            found[(dx, dy, dz)] = pltpu.make_async_remote_copy(
                src_ref=src, dst_ref=dst, send_sem=send.at[i], recv_sem=recv.at[i],
                device_id=device(dx, dy, dz), device_id_type=MESH)
        return found

    ALL = ((1, 0), (-1, 0), (0, 0), (1, 1), (1, -1), (-1, 1), (-1, -1), (0, 1), (0, -1))
    MAIN, CORN, SIDE = ALL[:3], ALL[3:7], ALL[7:]

    def each(found, sign, what, order=ALL):
        for dx, dy in order:
            if not any(d[:2] == (dx, dy) for d in found):
                continue

            def go(dx=dx, dy=dy):
                for dz in (0, 1, -1):
                    if (dx, dy, dz) in found:
                        getattr(found[(dx, dy, dz)], what)()
            guarded(inside(sign * dx, sign * dy), go)

    def lateral(rows_of, strips_of, flip, sink, lo, hi, off):
        def body(g, _):
            trow = pl.ds(pl.multiple_of(g * 8 + off, 8), 8)
            kx = [tb[KX + (6 - a if flip else a), trow, :] for a in range(7)]
            ky = [tb[KY + (6 - b if flip else b), trow, :] for b in range(7)]
            c, c1, c2 = strips_of(g)
            c1, c2 = jnp.where(lane < 96, c, c1), jnp.where(lane < 96, c, c2)
            al = kx[3] * c
            for a in (0, 1, 2, 4, 5, 6):
                al = al + kx[a] * pltpu.roll(c2 if a == 6 else c1, (18 - 6 * a) % 128, 1)
            sc = jnp.zeros((8, 128), F32)
            for b in (0, 1, 2, 4, 5, 6):
                ok = {0: lane6 >= 3, 1: jnp.logical_or(lane6 == 3, lane6 == 4), 2: lane6 == 3,
                      4: lane6 == 2, 5: jnp.logical_or(lane6 == 1, lane6 == 2), 6: lane6 <= 2}[b]
                sc = sc + jnp.where(ok, ky[b] * pltpu.roll(al, (R - b) % 128, 1), 0.0)
            window = [rows_of(x, g) for x in range(6)]
            along = []
            for x in range(NX):
                window.append(rows_of(x + 6, g))
                v = kx[0] * window[x]
                for a in range(1, 7):
                    v = v + kx[a] * window[x + a]
                along.append(v)
            hi, lo = split3(jnp.concatenate(along, axis=0))
            both = jnp.concatenate([hi, lo], axis=1)
            acc = [ky[R] * v for v in along]
            for n, (b0, b1) in enumerate(PAIRS):
                moved = jnp.dot(both, smat[n], preferred_element_type=F32)
                for x in range(NX):
                    acc[x] = acc[x] + ky[b0] * moved[8 * x : 8 * x + 8, 0:128] + ky[b1] * moved[8 * x : 8 * x + 8, 128:256]
            done = []
            for x in range(NX):
                done.append(acc[x] + jnp.where(edge, pltpu.roll(sc, (-(6 * x + R)) % 128, 1), 0.0))
            sink(g, done)
            return 0

        lax.fori_loop(lo, hi, body, 0)

    def rows_from(ref):
        return lambda x, g: ref[x, pl.ds(pl.multiple_of(g * 8, 8), 8), :]

    left = lane6 < R

    def strips_from(ref):
        def get(g):
            r = pl.ds(pl.multiple_of(g * 8, 8), 8)
            return jnp.where(left, ref[0, r, :], ref[1, r, :]), ch[0, r, :], ch[1, r, :]
        return get

    def band(i, j, k):
        row = stitch[pl.ds(jnp.clip(sx + i, 0, SX - 1), 1), pl.ds(jnp.clip(sy + j, 0, SY - 1), 1), :]
        return jnp.broadcast_to(row[0, :, k : k + 1], (8, 128))

    def half(pos, width):
        return jnp.where(pos < width, 0.5, 1.0).astype(F32)

    bands = {(i, j): (band(i, j, 0), band(i, j, 1)) for i in (-1, 0, 1) for j in (-1, 0, 1)}
    wrows = []
    for x in range(-R, NX + R):
        i = -1 if x < 0 else (1 if x >= NX else 0)
        row = half(jnp.full((8, 128), x - i * NX, jnp.int32), bands[i, 0][0]) * half(lane, bands[i, 0][1])
        cond = inside(i, 0)
        if cond is not None:
            row = row * jnp.where(cond, 1.0, 0.0).astype(F32)
        wrows.append(row)
    wpos = {0: lane // 6, -1: NX - R + (lane - 110) // 6, 1: (lane - 96) // 6}
    wstrips = []
    for i in (0, -1, 1):
        lane_i = (lane + 4) % 6 if i < 0 else lane6
        parts = []
        for j, pos in ((-1, NY - R + lane_i), (1, lane_i - R)):
            v = half(wpos[i], bands[i, j][0]) * half(pos, bands[i, j][1])
            parts.append(v * jnp.where(inside(i, j), 1.0, 0.0).astype(F32))
        wstrips.append(jnp.where(lane_i < R, parts[0], parts[1]))
    wstrips_at = (wstrips[0], jnp.where(lane < 110, wstrips[2], wstrips[1]), wstrips[2])

    total = psf[0]
    for j in range(1, 17):
        total = total + psf[j]

    def depth_matrix(m, k, forward):
        off = lax.broadcasted_iota(jnp.int32, (m, k), 1) - lax.broadcasted_iota(jnp.int32, (m, k), 0)
        h = jnp.zeros((m, k), F32)
        for j in range(17):
            h = jnp.where(off == j, psf[16 - j if forward else j], h)
        h = h / jnp.full((m, k), total, F32)
        hi = h.astype(BF16)
        lo = (h - hi.astype(F32)).astype(BF16)
        return jnp.concatenate([hi, hi, lo], axis=1)

    def split3(v):
        hi = v.astype(BF16)
        lo = (v - hi.astype(F32)).astype(BF16)
        return hi, lo

    nx = 3 - (sx == 0).astype(jnp.int32) - (sx == SX - 1).astype(jnp.int32)
    ny = 3 - (sy == 0).astype(jnp.int32) - (sy == SY - 1).astype(jnp.int32)
    for c in loads:
        c.wait()
    pl.semaphore_wait(barrier, nx * ny * 3 - 1)

    tcopies = [
        pltpu.make_async_remote_copy(
            src_ref=taps.at[pl.ds(s, HZ), :], dst_ref=taps.at[pl.ds(d, HZ), :],
            send_sem=t_sem.at[0, i], recv_sem=t_sem.at[1, i], device_id=device(0, 0, dz), device_id_type=MESH)
        for i, (dz, s, d) in enumerate(((1, NZ, 0), (-1, HZ, HZ + NZ)))
    ]
    for c in tcopies:
        c.start()
    e1 = copies(est1, ye1, pk.at[0], qe1, qk.at[0], HZ, DIRS, es1, er1)
    s1 = copies(spr1, ys1, pk.at[1], qs1, qk.at[1], 0, SDIRS, ss1, sr1)
    e2 = copies(est2, ye2, pk.at[2], qe2, qk.at[2], HZ, DIRS, es2, er2)
    s2 = copies(spr2, ys2, pk.at[3], qs2, qk.at[3], 0, SDIRS, ss2, sr2)

    def packed_groups(k):
        return [pk[k, 8 * g : 8 * g + 8, :] for g in range(NZ // 8)]

    each(e1, 1, "start", MAIN)
    pack_loop(est1, HZ, pk.at[0])
    pack_corners(packed_groups(0), qk.at[0])
    each(e1, 1, "start", CORN + SIDE)

    row = lax.broadcasted_iota(jnp.int32, (256, 128), 0) % 128
    col = lax.broadcasted_iota(jnp.int32, (256, 128), 1)
    for n, pair in enumerate(PAIRS):
        for k, b in enumerate(pair):
            smat[n, :, 128 * k : 128 * k + 128] = jnp.where(row == col + (b - R), 1.0, 0.0).astype(BF16)
    lax.fori_loop(2, 10, make_taps, 0)

    def reciprocal(v):
        r = pltpu.reciprocal(v, approx=True)
        return r * (2.0 - v * r)

    def keep_norm(g, values):
        for x, v in enumerate(values):
            rnorm[x, pl.ds(pl.multiple_of(g * 8, 8), 8), :] = reciprocal(v)

    lateral(lambda x, g: wrows[x], lambda g: wstrips_at, True, keep_norm, 0, NZ // 8, HZ)
    fwd1 = depth_matrix(48, 64, True)
    fwd2 = depth_matrix(32, 48, True)
    bwd = depth_matrix(64, 80, False)
    for c in tcopies:
        c.wait_recv()
    lax.fori_loop(0, 2, make_taps, 0)
    lax.fori_loop(10, 12, make_taps, 0)

    def keep_lest(g, values):
        for x, v in enumerate(values):
            lest[x, pl.ds(pl.multiple_of(g * 8, 8), 8), :] = v

    for est, ye, qe, ecop, spr, ys, qs, scop, pks, last in (
        (est1, ye1, qe1, e1, spr1, ys1, qs1, s1, 1, False),
        (est2, ye2, qe2, e2, spr2, ys2, qs2, s2, 3, True),
    ):
        each(ecop, -1, "wait_recv")
        unpack_corners(qe, HZ)
        lateral(rows_from(est), strips_from(ye), False, keep_lest, 0, EZ // 8, 0)
        strip = [jnp.zeros((8, 128), F32) for _ in range(NZ // 8)]
        for part in ((0, 1, 6, 7), (2, 3, 4, 5)):
            blurs = []
            for p in part:
                hi, lo = split3(jnp.concatenate([lest[2 * p], lest[2 * p + 1]], axis=1))
                top = jnp.concatenate([hi[0:64], lo[0:64], hi[0:64]], axis=0)
                low = jnp.concatenate([hi[48:96], lo[48:96], hi[48:96]], axis=0)
                blurs.append(jnp.concatenate(
                    [jnp.dot(fwd1, top, preferred_element_type=F32), jnp.dot(fwd2, low, preferred_element_type=F32)], axis=0))
            for p, blur in zip(part, blurs):
                a, b = 2 * p, 2 * p + 1
                wide = jnp.concatenate([wrows[R + a][0:1], wrows[R + b][0:1]], axis=1)
                seen = jnp.concatenate([est1[R + a, 8:88, :], est1[R + b, 8:88, :]], axis=1)
                hi, lo = split3(wide * seen * reciprocal(blur))
                back = jnp.dot(bwd, jnp.concatenate([hi, lo, hi], axis=0), preferred_element_type=F32)
                for x, v in ((a, back[:, 0:128]), (b, back[:, 128:256])):
                    spr[R + x] = v
                    strip = [place(t, v[8 * g : 8 * g + 8], x) for g, t in enumerate(strip)]
            if part[0] == 0:
                pack_corners(strip, qk.at[pks])
                each(scop, 1, "start", MAIN + CORN)
            else:
                for g, t in enumerate(strip):
                    pk[pks, 8 * g : 8 * g + 8, :] = t
        each(scop, 1, "start", SIDE)
        each(scop, -1, "wait_recv")
        unpack_corners(qs, 0)

        def keep_est(g, values, est=est, last=last):
            r = pl.ds(pl.multiple_of(g * 8, 8), 8)
            rz = pl.ds(pl.multiple_of(g * 8 + HZ, 8), 8)
            acc = jnp.zeros((8, 128), F32)
            for x, v in enumerate(values):
                new = est[R + x, rz, :] * v * rnorm[x, r, :]
                if last:
                    res[x, r, :] = new
                else:
                    est2[R + x, rz, :] = new
                    acc = place(acc, new, x)
            if not last:
                pk[2, r, :] = acc

        lateral(rows_from(spr), strips_from(ys), True, keep_est, 0, NZ // 8, HZ)
        if not last:
            each(e2, 1, "start", MAIN)
            pack_corners(packed_groups(2), qk.at[2])
            each(e2, 1, "start", CORN + SIDE)

    stores = [pltpu.make_async_copy(res.at[x], out.at[:, x, :], out_sem.at[x]) for x in range(NX)]
    for c in stores:
        c.start()
    for c in tcopies:
        c.wait_send()
    for found in (e1, s1, e2, s2):
        each(found, 1, "wait_send")
    for c in stores:
        c.wait()


def body(observed, zone_of_slice, lateral_x, lateral_y, depth_psf, stitch_width):
    hbm = pl.BlockSpec(memory_space=pltpu.HBM)
    smem = pl.BlockSpec(memory_space=pltpu.SMEM)
    vmem = pl.BlockSpec(memory_space=pltpu.VMEM)
    dma = pltpu.SemaphoreType.DMA
    ne, ns = len(DIRS), len(SDIRS)
    return pl.pallas_call(
        kernel,
        out_shape=jax.ShapeDtypeStruct(observed.shape, F32),
        in_specs=[hbm, smem, vmem, vmem, smem, vmem],
        out_specs=hbm,
        scratch_shapes=[
            pltpu.VMEM((EX, EZ, NY), F32), pltpu.VMEM((EX, EZ, NY), F32),
            pltpu.VMEM((EX, NZ, NY), F32), pltpu.VMEM((EX, NZ, NY), F32),
            pltpu.VMEM((4, NZ, 128), F32), pltpu.VMEM((4, 4, 8, 128), F32),
            pltpu.VMEM((2, EZ, 128), F32), pltpu.VMEM((2, EZ, 128), F32),
            pltpu.VMEM((2, NZ, 128), F32), pltpu.VMEM((2, NZ, 128), F32),
            pltpu.VMEM((2, 2, 3, 8, 128), F32), pltpu.VMEM((2, 2, 3, 8, 128), F32),
            pltpu.VMEM((2, 2, 3, 8, 128), F32), pltpu.VMEM((2, 2, 3, 8, 128), F32),
            pltpu.VMEM((2, EZ, 128), F32),
            pltpu.VMEM((NX, EZ, NY), F32), pltpu.VMEM((NX, NZ, NY), F32), pltpu.VMEM((NX, NZ, NY), F32),
            pltpu.VMEM((8, 128), F32), pltpu.VMEM((EZ, 128), F32), pltpu.VMEM((14, EZ, 128), F32),
            pltpu.VMEM((3, 256, 256), BF16),
            dma((NX,)), dma((NX,)), dma((2, 2)),
            dma((ne,)), dma((ne,)), dma((ne,)), dma((ne,)),
            dma((ns,)), dma((ns,)), dma((ns,)), dma((ns,)),
        ],
        compiler_params=pltpu.CompilerParams(collective_id=0, has_side_effects=True, vmem_limit_bytes=40 * 1024 * 1024),
        name="deconvolve",
    )(observed, zone_of_slice, lateral_x, lateral_y, depth_psf, stitch_width)


def solution(mesh):
    in_specs = (P("gz", "sx", "sy"), P("gz"), P(), P(), P(), P())
    out_specs = P("gz", "sx", "sy")
    return jax.shard_map(body, mesh=mesh, in_specs=in_specs, out_specs=out_specs, check_vma=False)
```

```python
import itertools
import jax
import jax.numpy as jnp
from jax import lax
from jax.experimental import pallas as pl
from jax.experimental.pallas import tpu as pltpu
from jax.sharding import PartitionSpec as P

MESH = pl.DeviceIdType.MESH
F32 = jnp.float32
BF16 = jnp.bfloat16
NX, NY, NZ = 16, 128, 64
R = 3
HZ = 16
EZ = NZ + 2 * HZ
EX = NX + 2 * R
SX, SY, GZ = 4, 4, 8
DIRS = [d for d in itertools.product((-1, 0, 1), repeat=3) if d != (0, 0, 0)]
SDIRS = [d for d in DIRS if d[2] == 0]
KX, KY = 0, 7
UNROLL = 4
PAIRS = ((0, 1), (2, 4), (5, 6))
CORNERS = {(1, 1): (78, 110), (1, -1): (81, 113), (-1, 1): (0, 96), (-1, -1): (3, 99)}


def kernel(
    obs, zone, lat_x, lat_y, psf, stitch, out,
    est1, est2, spr1, spr2, pk, qk, ye1, ye2, ys1, ys2, qe1, qe2, qs1, qs2, ch, lest, rnorm, res,
    ktab, taps, tb, smat, scr, in_sem, out_sem, t_sem,
    es1, er1, es2, er2, ss1, sr1, ss2, sr2,
):
    sx, sy, gz = lax.axis_index("sx"), lax.axis_index("sy"), lax.axis_index("gz")
    lane = lax.broadcasted_iota(jnp.int32, (8, 128), 1)
    lane6 = lane % 6
    edge = jnp.logical_or(lane < R, lane >= NY - R)

    loads = [pltpu.make_async_copy(obs.at[:, x, :], est1.at[R + x, pl.ds(HZ, NZ)], in_sem.at[x]) for x in range(NX)]
    for c in loads:
        c.start()

    def inside(dx, dy):
        ok = None
        for at, d, n in ((sx, dx, SX), (sy, dy, SY)):
            if d:
                t = at < n - 1 if d > 0 else at > 0
                ok = t if ok is None else jnp.logical_and(ok, t)
        return ok

    def guarded(cond, fn):
        if cond is None:
            fn()
        else:
            pl.when(cond)(fn)

    def device(dx, dy, dz):
        return (sx + dx, sy + dy, lax.rem(gz + dz + GZ, GZ))

    for dx, slot, rows in ((1, 0, 0), (-1, 1, EX - R)):
        @pl.when(jnp.logical_not(inside(-dx, 0)))
        def _(slot=slot, rows=rows):
            for e in (est1, est2, spr1, spr2):
                e[pl.ds(rows, R)] = jnp.zeros((R,) + e.shape[1:], F32)
            for q in (qe1, qe2, qs1, qs2):
                for side in range(2):
                    q[side, slot] = jnp.zeros(q.shape[2:], F32)
    for dy, side in ((1, 0), (-1, 1)):
        @pl.when(jnp.logical_not(inside(0, -dy)))
        def _(side=side):
            for y in (ye1, ye2, ys1, ys2, qe1, qe2, qs1, qs2):
                y[side] = jnp.zeros(y.shape[1:], F32)

    barrier = pltpu.get_barrier_semaphore()
    for dx, dy in itertools.product((-1, 0, 1), repeat=2):
        def greet(dx=dx, dy=dy):
            for dz in (-1, 0, 1):
                if (dx, dy, dz) != (0, 0, 0):
                    pl.semaphore_signal(barrier, inc=1, device_id=device(dx, dy, dz), device_id_type=MESH)
        guarded(inside(dx, dy), greet)

    ktab[...] = jnp.zeros((8, 128), F32)
    ktab[:, 0:7] = lat_x[...]
    ktab[:, 7:14] = lat_y[...]
    for z in range(NZ):
        taps[HZ + z : HZ + z + 1, :] = ktab[pl.ds(zone[z], 1), :]

    def make_taps(g, _):
        rows = pl.ds(pl.multiple_of(g * 8, 8), 8)
        t = taps[rows, :]
        for i in range(14):
            tb[i, rows, :] = jnp.broadcast_to(t[:, i : i + 1], (8, 128))
        return 0


    def place(acc, v, x):
        at = jnp.logical_and(lane >= 6 * x, lane < 6 * x + 6)
        return jnp.where(at, pltpu.roll(v, 6 * x + R, 1), acc)

    def pack_loop(src, off, dst):
        def body(g, _):
            acc = jnp.zeros((8, 128), F32)
            for x in range(NX):
                acc = place(acc, src[R + x, pl.ds(pl.multiple_of(g * 8 + off, 8), 8), :], x)
            dst[pl.ds(pl.multiple_of(g * 8, 8), 8), :] = acc
            return 0

        lax.fori_loop(0, NZ // 8, body, 0)

    def pack_corners(groups, dst):
        for k, (first, _) in enumerate(CORNERS.values()):
            acc = jnp.zeros((8, 128), F32)
            for g in range(NZ // 8):
                at = jnp.logical_and(lane >= 16 * g, lane < 16 * g + 16)
                acc = jnp.where(at, pltpu.roll(groups[g], (16 * g - first) % 128, 1), acc)
            dst[k] = acc

    def unpack_corners(src, halo):
        up = (lane + 4) % 6 < R
        for g in range((NZ + 2 * halo) // 8):
            slot, local = 1, g - halo // 8
            if local < 0:
                slot, local = 0, local + NZ // 8
            elif local >= NZ // 8:
                slot, local = 2, local - NZ // 8
            got = [pltpu.roll(src[0 if d[1] > 0 else 1, 0 if d[0] > 0 else 1, slot], (at - 16 * local) % 128, 1)
                   for d, (_, at) in CORNERS.items()]
            cu = jnp.where(up, got[0], got[1])
            cd = jnp.where(left, got[2], got[3])
            ch[0, g * 8 : g * 8 + 8, :] = jnp.where(lane < 110, cd, cu)
            ch[1, g * 8 : g * 8 + 8, :] = cd

    def copies(main, strips, packed, corners, cpacked, halo, dirs, send, recv):
        found = {}
        for i, (dx, dy, dz) in enumerate(dirs):
            zs, zd, n = {0: (0, halo, NZ), 1: (NZ - HZ, 0, HZ), -1: (0, halo + NZ, HZ)}[dz]
            if dy == 0:
                xs, xd, m = {0: (R, R, NX), 1: (NX, 0, R), -1: (R, R + NX, R)}[dx]
                src = main.at[pl.ds(xs, m), pl.ds(halo + zs, n), :]
                dst = main.at[pl.ds(xd, m), pl.ds(zd, n), :]
            elif dx == 0:
                src = packed.at[pl.ds(zs, n), :]
                dst = strips.at[0 if dy > 0 else 1, pl.ds(zd, n), :]
            else:
                src = cpacked.at[list(CORNERS).index((dx, dy))]
                dst = corners.at[0 if dy > 0 else 1, 0 if dx > 0 else 1, 1 - dz]
            found[(dx, dy, dz)] = pltpu.make_async_remote_copy(
                src_ref=src, dst_ref=dst, send_sem=send.at[i], recv_sem=recv.at[i],
                device_id=device(dx, dy, dz), device_id_type=MESH)
        return found

    ALL = ((1, 0), (-1, 0), (0, 0), (1, 1), (1, -1), (-1, 1), (-1, -1), (0, 1), (0, -1))
    MAIN, CORN, SIDE = ALL[:3], ALL[3:7], ALL[7:]

    def each(found, sign, what, order=ALL):
        for dx, dy in order:
            if not any(d[:2] == (dx, dy) for d in found):
                continue

            def go(dx=dx, dy=dy):
                for dz in (0, 1, -1):
                    if (dx, dy, dz) in found:
                        getattr(found[(dx, dy, dz)], what)()
            guarded(inside(sign * dx, sign * dy), go)

    def lateral(rows_of, strips_of, flip, sink, lo, hi, off):
        def taps_at(g):
            trow = pl.ds(pl.multiple_of(g * 8 + off, 8), 8)
            return ([tb[KX + (6 - a if flip else a), trow, :] for a in range(7)],
                    [tb[KY + (6 - b if flip else b), trow, :] for b in range(7)])

        for g in range(lo, hi):
            kx, ky = taps_at(g)
            c, c1, c2 = strips_of(g)
            c1, c2 = jnp.where(lane < 96, c, c1), jnp.where(lane < 96, c, c2)
            al = kx[3] * c
            for a in (0, 1, 2, 4, 5, 6):
                al = al + kx[a] * pltpu.roll(c2 if a == 6 else c1, (18 - 6 * a) % 128, 1)
            sc = jnp.zeros((8, 128), F32)
            for b in (0, 1, 2, 4, 5, 6):
                ok = {0: lane6 >= 3, 1: jnp.logical_or(lane6 == 3, lane6 == 4), 2: lane6 == 3,
                      4: lane6 == 2, 5: jnp.logical_or(lane6 == 1, lane6 == 2), 6: lane6 <= 2}[b]
                sc = sc + jnp.where(ok, ky[b] * pltpu.roll(al, (R - b) % 128, 1), 0.0)
            scr[8 * g : 8 * g + 8, :] = sc

        def group(g):
            kx, ky = taps_at(g)
            sc = scr[pl.ds(pl.multiple_of(g * 8, 8), 8), :]
            window = [rows_of(x, g) for x in range(6)]
            along = []
            for x in range(NX):
                window.append(rows_of(x + 6, g))
                v = kx[0] * window[x]
                for a in range(1, 7):
                    v = v + kx[a] * window[x + a]
                along.append(v)
            hi, lo = split3(jnp.concatenate(along, axis=0))
            both = jnp.concatenate([hi, lo], axis=1)
            acc = [ky[R] * v + jnp.where(edge, pltpu.roll(sc, (-(6 * x + R)) % 128, 1), 0.0) for x, v in enumerate(along)]
            for n, (b0, b1) in enumerate(PAIRS):
                moved = jnp.dot(both, smat[n], preferred_element_type=F32)
                for x in range(NX):
                    acc[x] = acc[x] + ky[b0] * moved[8 * x : 8 * x + 8, 0:128] + ky[b1] * moved[8 * x : 8 * x + 8, 128:256]
            sink(g, acc)

        def body(i, _):
            for k in range(UNROLL):
                group(lo + i * UNROLL + k)
            return 0

        lax.fori_loop(0, (hi - lo) // UNROLL, body, 0)

    def rows_from(ref):
        return lambda x, g: ref[x, pl.ds(pl.multiple_of(g * 8, 8), 8), :]

    left = lane6 < R

    def strips_from(ref):
        def get(g):
            r = pl.ds(pl.multiple_of(g * 8, 8), 8)
            return jnp.where(left, ref[0, r, :], ref[1, r, :]), ch[0, r, :], ch[1, r, :]
        return get

    def band(i, j, k):
        row = stitch[pl.ds(jnp.clip(sx + i, 0, SX - 1), 1), pl.ds(jnp.clip(sy + j, 0, SY - 1), 1), :]
        return jnp.broadcast_to(row[0, :, k : k + 1], (8, 128))

    def half(pos, width):
        return jnp.where(pos < width, 0.5, 1.0).astype(F32)

    bands = {(i, j): (band(i, j, 0), band(i, j, 1)) for i in (-1, 0, 1) for j in (-1, 0, 1)}
    wrows = []
    for x in range(-R, NX + R):
        i = -1 if x < 0 else (1 if x >= NX else 0)
        row = half(jnp.full((8, 128), x - i * NX, jnp.int32), bands[i, 0][0]) * half(lane, bands[i, 0][1])
        cond = inside(i, 0)
        if cond is not None:
            row = row * jnp.where(cond, 1.0, 0.0).astype(F32)
        wrows.append(row)
    wpos = {0: lane // 6, -1: NX - R + (lane - 110) // 6, 1: (lane - 96) // 6}
    wstrips = []
    for i in (0, -1, 1):
        lane_i = (lane + 4) % 6 if i < 0 else lane6
        parts = []
        for j, pos in ((-1, NY - R + lane_i), (1, lane_i - R)):
            v = half(wpos[i], bands[i, j][0]) * half(pos, bands[i, j][1])
            parts.append(v * jnp.where(inside(i, j), 1.0, 0.0).astype(F32))
        wstrips.append(jnp.where(lane_i < R, parts[0], parts[1]))
    wstrips_at = (wstrips[0], jnp.where(lane < 110, wstrips[2], wstrips[1]), wstrips[2])

    total = psf[0]
    for j in range(1, 17):
        total = total + psf[j]

    def depth_matrix(m, k, forward):
        off = lax.broadcasted_iota(jnp.int32, (m, k), 1) - lax.broadcasted_iota(jnp.int32, (m, k), 0)
        h = jnp.zeros((m, k), F32)
        for j in range(17):
            h = jnp.where(off == j, psf[16 - j if forward else j], h)
        h = h / jnp.full((m, k), total, F32)
        hi = h.astype(BF16)
        lo = (h - hi.astype(F32)).astype(BF16)
        return jnp.concatenate([hi, hi, lo], axis=1)

    def split3(v):
        hi = v.astype(BF16)
        lo = (v - hi.astype(F32)).astype(BF16)
        return hi, lo

    nx = 3 - (sx == 0).astype(jnp.int32) - (sx == SX - 1).astype(jnp.int32)
    ny = 3 - (sy == 0).astype(jnp.int32) - (sy == SY - 1).astype(jnp.int32)
    for c in loads:
        c.wait()
    pl.semaphore_wait(barrier, nx * ny * 3 - 1)

    tcopies = [
        pltpu.make_async_remote_copy(
            src_ref=taps.at[pl.ds(s, HZ), :], dst_ref=taps.at[pl.ds(d, HZ), :],
            send_sem=t_sem.at[0, i], recv_sem=t_sem.at[1, i], device_id=device(0, 0, dz), device_id_type=MESH)
        for i, (dz, s, d) in enumerate(((1, NZ, 0), (-1, HZ, HZ + NZ)))
    ]
    for c in tcopies:
        c.start()
    e1 = copies(est1, ye1, pk.at[0], qe1, qk.at[0], HZ, DIRS, es1, er1)
    s1 = copies(spr1, ys1, pk.at[1], qs1, qk.at[1], 0, SDIRS, ss1, sr1)
    e2 = copies(est2, ye2, pk.at[2], qe2, qk.at[2], HZ, DIRS, es2, er2)
    s2 = copies(spr2, ys2, pk.at[3], qs2, qk.at[3], 0, SDIRS, ss2, sr2)

    def packed_groups(k):
        return [pk[k, 8 * g : 8 * g + 8, :] for g in range(NZ // 8)]

    each(e1, 1, "start", MAIN)
    pack_loop(est1, HZ, pk.at[0])
    pack_corners(packed_groups(0), qk.at[0])
    each(e1, 1, "start", CORN + SIDE)

    row = lax.broadcasted_iota(jnp.int32, (256, 128), 0) % 128
    col = lax.broadcasted_iota(jnp.int32, (256, 128), 1)
    for n, pair in enumerate(PAIRS):
        for k, b in enumerate(pair):
            smat[n, :, 128 * k : 128 * k + 128] = jnp.where(row == col + (b - R), 1.0, 0.0).astype(BF16)
    lax.fori_loop(2, 10, make_taps, 0)

    def reciprocal(v):
        r = pltpu.reciprocal(v, approx=True)
        return r * (2.0 - v * r)

    def keep_norm(g, values):
        for x, v in enumerate(values):
            rnorm[x, pl.ds(pl.multiple_of(g * 8, 8), 8), :] = reciprocal(v)

    lateral(lambda x, g: wrows[x], lambda g: wstrips_at, True, keep_norm, 0, NZ // 8, HZ)
    fwd1 = depth_matrix(48, 64, True)
    fwd2 = depth_matrix(32, 48, True)
    bwd = depth_matrix(64, 80, False)
    for c in tcopies:
        c.wait_recv()
    lax.fori_loop(0, 2, make_taps, 0)
    lax.fori_loop(10, 12, make_taps, 0)

    def keep_lest(g, values):
        for x, v in enumerate(values):
            lest[x, pl.ds(pl.multiple_of(g * 8, 8), 8), :] = v

    for est, ye, qe, ecop, spr, ys, qs, scop, pks, last in (
        (est1, ye1, qe1, e1, spr1, ys1, qs1, s1, 1, False),
        (est2, ye2, qe2, e2, spr2, ys2, qs2, s2, 3, True),
    ):
        each(ecop, -1, "wait_recv")
        unpack_corners(qe, HZ)
        lateral(rows_from(est), strips_from(ye), False, keep_lest, 0, EZ // 8, 0)
        strip = [jnp.zeros((8, 128), F32) for _ in range(NZ // 8)]
        for part in ((0, 1, 6, 7), (2, 3, 4, 5)):
            blurs = []
            for p in part:
                hi, lo = split3(jnp.concatenate([lest[2 * p], lest[2 * p + 1]], axis=1))
                top = jnp.concatenate([hi[0:64], lo[0:64], hi[0:64]], axis=0)
                low = jnp.concatenate([hi[48:96], lo[48:96], hi[48:96]], axis=0)
                blurs.append(jnp.concatenate(
                    [jnp.dot(fwd1, top, preferred_element_type=F32), jnp.dot(fwd2, low, preferred_element_type=F32)], axis=0))
            for p, blur in zip(part, blurs):
                a, b = 2 * p, 2 * p + 1
                wide = jnp.concatenate([wrows[R + a][0:1], wrows[R + b][0:1]], axis=1)
                seen = jnp.concatenate([est1[R + a, 8:88, :], est1[R + b, 8:88, :]], axis=1)
                hi, lo = split3(wide * seen * reciprocal(blur))
                back = jnp.dot(bwd, jnp.concatenate([hi, lo, hi], axis=0), preferred_element_type=F32)
                for x, v in ((a, back[:, 0:128]), (b, back[:, 128:256])):
                    spr[R + x] = v
                    strip = [place(t, v[8 * g : 8 * g + 8], x) for g, t in enumerate(strip)]
            if part[0] == 0:
                pack_corners(strip, qk.at[pks])
                each(scop, 1, "start", MAIN + CORN)
            else:
                for g, t in enumerate(strip):
                    pk[pks, 8 * g : 8 * g + 8, :] = t
        each(scop, 1, "start", SIDE)
        each(scop, -1, "wait_recv")
        unpack_corners(qs, 0)

        def keep_est(g, values, est=est, last=last):
            r = pl.ds(pl.multiple_of(g * 8, 8), 8)
            rz = pl.ds(pl.multiple_of(g * 8 + HZ, 8), 8)
            acc = jnp.zeros((8, 128), F32)
            for x, v in enumerate(values):
                new = est[R + x, rz, :] * v * rnorm[x, r, :]
                if last:
                    res[x, r, :] = new
                else:
                    est2[R + x, rz, :] = new
                    acc = place(acc, new, x)
            if not last:
                pk[2, r, :] = acc

        lateral(rows_from(spr), strips_from(ys), True, keep_est, 0, NZ // 8, HZ)
        if not last:
            each(e2, 1, "start", MAIN)
            pack_corners(packed_groups(2), qk.at[2])
            each(e2, 1, "start", CORN + SIDE)

    stores = [pltpu.make_async_copy(res.at[x], out.at[:, x, :], out_sem.at[x]) for x in range(NX)]
    for c in stores:
        c.start()
    for c in tcopies:
        c.wait_send()
    for found in (e1, s1, e2, s2):
        each(found, 1, "wait_send")
    for c in stores:
        c.wait()


def body(observed, zone_of_slice, lateral_x, lateral_y, depth_psf, stitch_width):
    hbm = pl.BlockSpec(memory_space=pltpu.HBM)
    smem = pl.BlockSpec(memory_space=pltpu.SMEM)
    vmem = pl.BlockSpec(memory_space=pltpu.VMEM)
    dma = pltpu.SemaphoreType.DMA
    ne, ns = len(DIRS), len(SDIRS)
    return pl.pallas_call(
        kernel,
        out_shape=jax.ShapeDtypeStruct(observed.shape, F32),
        in_specs=[hbm, smem, vmem, vmem, smem, vmem],
        out_specs=hbm,
        scratch_shapes=[
            pltpu.VMEM((EX, EZ, NY), F32), pltpu.VMEM((EX, EZ, NY), F32),
            pltpu.VMEM((EX, NZ, NY), F32), pltpu.VMEM((EX, NZ, NY), F32),
            pltpu.VMEM((4, NZ, 128), F32), pltpu.VMEM((4, 4, 8, 128), F32),
            pltpu.VMEM((2, EZ, 128), F32), pltpu.VMEM((2, EZ, 128), F32),
            pltpu.VMEM((2, NZ, 128), F32), pltpu.VMEM((2, NZ, 128), F32),
            pltpu.VMEM((2, 2, 3, 8, 128), F32), pltpu.VMEM((2, 2, 3, 8, 128), F32),
            pltpu.VMEM((2, 2, 3, 8, 128), F32), pltpu.VMEM((2, 2, 3, 8, 128), F32),
            pltpu.VMEM((2, EZ, 128), F32),
            pltpu.VMEM((NX, EZ, NY), F32), pltpu.VMEM((NX, NZ, NY), F32), pltpu.VMEM((NX, NZ, NY), F32),
            pltpu.VMEM((8, 128), F32), pltpu.VMEM((EZ, 128), F32), pltpu.VMEM((14, EZ, 128), F32),
            pltpu.VMEM((3, 256, 256), BF16), pltpu.VMEM((EZ, 128), F32),
            dma((NX,)), dma((NX,)), dma((2, 2)),
            dma((ne,)), dma((ne,)), dma((ne,)), dma((ne,)),
            dma((ns,)), dma((ns,)), dma((ns,)), dma((ns,)),
        ],
        compiler_params=pltpu.CompilerParams(collective_id=0, has_side_effects=True, vmem_limit_bytes=40 * 1024 * 1024),
        name="deconvolve",
    )(observed, zone_of_slice, lateral_x, lateral_y, depth_psf, stitch_width)


def solution(mesh):
    in_specs = (P("gz", "sx", "sy"), P("gz"), P(), P(), P(), P())
    out_specs = P("gz", "sx", "sy")
    return jax.shard_map(body, mesh=mesh, in_specs=in_specs, out_specs=out_specs, check_vma=False)
```

```python
import itertools
import jax
import jax.numpy as jnp
from jax import lax
from jax.experimental import pallas as pl
from jax.experimental.pallas import tpu as pltpu
from jax.sharding import PartitionSpec as P

MESH = pl.DeviceIdType.MESH
F32 = jnp.float32
BF16 = jnp.bfloat16
NX, NY, NZ = 16, 128, 64
R = 3
HZ = 16
EZ = NZ + 2 * HZ
EX = NX + 2 * R
SX, SY, GZ = 4, 4, 8
DIRS = [d for d in itertools.product((-1, 0, 1), repeat=3) if d != (0, 0, 0)]
DIRS += [(1, 0, 2), (-1, 0, 2)]
SDIRS = [d for d in DIRS if d[2] in (0, 2)]
KX, KY, KF, KB = 0, 7, 14, 20
EDGE = (0, 1, 2, 13, 14, 15)
INNER = tuple(range(3, 13))
PAIRS = ((0, 1), (2, 4), (5, 6))
CORNERS = {(1, 1): (78, 110), (1, -1): (81, 113), (-1, 1): (0, 96), (-1, -1): (3, 99)}


def kernel(
    obs, zone, lat_x, lat_y, psf, stitch, out,
    est1, est2, spr1, spr2, pk, qk, ye1, ye2, ys1, ys2, qe1, qe2, qs1, qs2, ch, lest, rnorm, res,
    ktab, taps, tb, smat, scr, pmain, pnorm, in_sem, out_sem, t_sem,
    es1, er1, es2, er2, ss1, sr1, ss2, sr2,
):
    sx, sy, gz = lax.axis_index("sx"), lax.axis_index("sy"), lax.axis_index("gz")
    lane = lax.broadcasted_iota(jnp.int32, (8, 128), 1)
    lane6 = lane % 6
    edge = jnp.logical_or(lane < R, lane >= NY - R)
    lane_all = lax.broadcasted_iota(jnp.int32, (EZ, 128), 1)
    edge_all = jnp.logical_or(lane_all < R, lane_all >= NY - R)

    loads = [pltpu.make_async_copy(obs.at[:, x, :], est1.at[R + x, pl.ds(HZ, NZ)], in_sem.at[x]) for x in range(NX)]
    for c in loads:
        c.start()

    def inside(dx, dy):
        ok = None
        for at, d, n in ((sx, dx, SX), (sy, dy, SY)):
            if d:
                t = at < n - 1 if d > 0 else at > 0
                ok = t if ok is None else jnp.logical_and(ok, t)
        return ok

    def guarded(cond, fn):
        if cond is None:
            fn()
        else:
            pl.when(cond)(fn)

    def device(dx, dy, dz):
        return (sx + dx, sy + dy, lax.rem(gz + dz + GZ, GZ))

    for dx, slot, rows in ((1, 0, 0), (-1, 1, EX - R)):
        @pl.when(jnp.logical_not(inside(-dx, 0)))
        def _(slot=slot, rows=rows):
            for e in (est1, est2, spr1, spr2):
                e[pl.ds(rows, R)] = jnp.zeros((R,) + e.shape[1:], F32)
            for q in (qe1, qe2, qs1, qs2):
                for side in range(2):
                    q[side, slot] = jnp.zeros(q.shape[2:], F32)
    for dy, side in ((1, 0), (-1, 1)):
        @pl.when(jnp.logical_not(inside(0, -dy)))
        def _(side=side):
            for y in (ye1, ye2, ys1, ys2, qe1, qe2, qs1, qs2):
                y[side] = jnp.zeros(y.shape[1:], F32)

    barrier = pltpu.get_barrier_semaphore()
    for dx, dy in itertools.product((-1, 0, 1), repeat=2):
        def greet(dx=dx, dy=dy):
            for dz in (-1, 0, 1):
                if (dx, dy, dz) != (0, 0, 0):
                    pl.semaphore_signal(barrier, inc=1, device_id=device(dx, dy, dz), device_id_type=MESH)
        guarded(inside(dx, dy), greet)

    def make_taps(g, _):
        rows = pl.ds(pl.multiple_of(g * 8, 8), 8)
        t = taps[rows, :]
        for i in range(14):
            tb[i, rows, :] = jnp.broadcast_to(t[:, i : i + 1], (8, 128))
        for k, b in enumerate((0, 1, 2, 4, 5, 6)):
            ok = {0: lane6 >= 3, 1: jnp.logical_or(lane6 == 3, lane6 == 4), 2: lane6 == 3,
                  4: lane6 == 2, 5: jnp.logical_or(lane6 == 1, lane6 == 2), 6: lane6 <= 2}[b]
            tb[KF + k, rows, :] = jnp.where(ok, jnp.broadcast_to(t[:, 7 + b : 8 + b], (8, 128)), 0.0)
            tb[KB + k, rows, :] = jnp.where(ok, jnp.broadcast_to(t[:, 13 - b : 14 - b], (8, 128)), 0.0)
        return 0


    def place(acc, v, x):
        at = jnp.logical_and(lane >= 6 * x, lane < 6 * x + 6)
        return jnp.where(at, pltpu.roll(v, 6 * x + R, 1), acc)

    def pack_block(src, off, dst):
        for g in range(NZ // 8):
            acc = jnp.zeros((8, 128), F32)
            for x in range(NX):
                acc = place(acc, src[R + x, g * 8 + off : g * 8 + off + 8, :], x)
            dst[g * 8 : g * 8 + 8, :] = acc

    def pack_corners(groups, dst):
        for k, (first, _) in enumerate(CORNERS.values()):
            acc = jnp.zeros((8, 128), F32)
            for g in range(NZ // 8):
                at = jnp.logical_and(lane >= 16 * g, lane < 16 * g + 16)
                acc = jnp.where(at, pltpu.roll(groups[g], (16 * g - first) % 128, 1), acc)
            dst[k] = acc

    def unpack_corners(src, halo):
        up = (lane + 4) % 6 < R
        for g in range((NZ + 2 * halo) // 8):
            slot, local = 1, g - halo // 8
            if local < 0:
                slot, local = 0, local + NZ // 8
            elif local >= NZ // 8:
                slot, local = 2, local - NZ // 8
            got = [pltpu.roll(src[0 if d[1] > 0 else 1, 0 if d[0] > 0 else 1, slot], (at - 16 * local) % 128, 1)
                   for d, (_, at) in CORNERS.items()]
            cu = jnp.where(up, got[0], got[1])
            cd = jnp.where(left, got[2], got[3])
            ch[0, g * 8 : g * 8 + 8, :] = jnp.where(lane < 110, cd, cu)
            ch[1, g * 8 : g * 8 + 8, :] = cd

    def copies(main, strips, packed, corners, cpacked, halo, dirs, send, recv):
        found = {}
        for i, (dx, dy, dz) in enumerate(dirs):
            zs, zd, n = {0: (0, halo, NZ), 1: (NZ - HZ, 0, HZ), -1: (0, halo + NZ, HZ), 2: (NZ // 2, halo + NZ // 2, NZ // 2)}[dz]
            if dx and not dy and dz == 0:
                n = NZ // 2
            if dy == 0:
                xs, xd, m = {0: (R, R, NX), 1: (NX, 0, R), -1: (R, R + NX, R)}[dx]
                src = main.at[pl.ds(xs, m), pl.ds(halo + zs, n), :]
                dst = main.at[pl.ds(xd, m), pl.ds(zd, n), :]
            elif dx == 0:
                src = packed.at[pl.ds(zs, n), :]
                dst = strips.at[0 if dy > 0 else 1, pl.ds(zd, n), :]
            else:
                src = cpacked.at[list(CORNERS).index((dx, dy))]
                dst = corners.at[0 if dy > 0 else 1, 0 if dx > 0 else 1, 1 - dz]
            found[(dx, dy, dz)] = pltpu.make_async_remote_copy(
                src_ref=src, dst_ref=dst, send_sem=send.at[i], recv_sem=recv.at[i],
                device_id=device(dx, dy, 0 if dz == 2 else dz), device_id_type=MESH)
        return found

    X_LOW, X_HIGH = [(1, 0, 0), (-1, 0, 0)], [(1, 0, 2), (-1, 0, 2)]
    X_FACE, Z_FACE, Y_FACE = X_LOW + X_HIGH, [(0, 0, 1), (0, 0, -1)], [(0, 1, 0), (0, -1, 0)]
    XZ = [(dx, 0, dz) for dx in (1, -1) for dz in (1, -1)]
    YZ = [(0, dy, dz) for dy in (1, -1) for dz in (1, -1)]
    CORN = [(dx, dy, dz) for dx in (1, -1) for dy in (1, -1) for dz in (0, 1, -1)]
    XS = XZ + X_LOW + X_HIGH
    SIDES = [(0, dy, dz) for dy in (1, -1) for dz in (1, -1, 0)]

    def each(found, sign, what, which):
        for (dx, dy), ds in itertools.groupby([d for d in which if d in found], key=lambda d: d[:2]):
            def go(ds=tuple(ds)):
                for d in ds:
                    getattr(found[d], what)()
            guarded(inside(sign * dx, sign * dy), go)

    def taps_at(g, flip, off):
        trow = pl.ds(pl.multiple_of(g * 8 + off, 8), 8)
        return ([tb[KX + (6 - a if flip else a), trow, :] for a in range(7)],
                [tb[KY + (6 - b if flip else b), trow, :] for b in range(7)])

    def halo_strips(c, c1, c2, flip, off):
        n = c.shape[0]
        rows = slice(off, off + n)
        own = lane_all[:n] < 96
        c1, c2 = jnp.where(own, c, c1), jnp.where(own, c, c2)
        al = tb[KX + 3, rows, :] * c
        for a in (0, 1, 2, 4, 5, 6):
            al = al + tb[KX + (6 - a if flip else a), rows, :] * pltpu.roll(c2 if a == 6 else c1, (18 - 6 * a) % 128, 1)
        sc = None
        for k, b in enumerate((0, 1, 2, 4, 5, 6)):
            v = tb[(KB if flip else KF) + k, rows, :] * pltpu.roll(al, (R - b) % 128, 1)
            sc = v if sc is None else sc + v
        scr[0:n, :] = sc

    def conv(rows_of, flip, xs, lo, hi, off, fuse, unroll, sink):
        def part(first):
            groups = [first + k for k in range(fuse)]
            along, taps_y = [], []
            for g in groups:
                kx, ky = taps_at(g, flip, off)
                taps_y.append(ky)
                rows = {}
                for x in xs:
                    for a in range(7):
                        if x + a not in rows:
                            rows[x + a] = rows_of(x + a, g)
                    v = kx[0] * rows[x]
                    for a in range(1, 7):
                        v = v + kx[a] * rows[x + a]
                    along.append(v)
            hi, lo_ = split3(jnp.concatenate(along, axis=0))
            both = jnp.concatenate([hi, lo_], axis=1)
            n = len(xs)
            acc = [taps_y[k // n][R] * v for k, v in enumerate(along)]
            for m, (b0, b1) in enumerate(PAIRS):
                moved = jnp.dot(both, smat[m], preferred_element_type=F32)
                for k in range(len(acc)):
                    ky = taps_y[k // n]
                    acc[k] = acc[k] + ky[b0] * moved[8 * k : 8 * k + 8, 0:128] + ky[b1] * moved[8 * k : 8 * k + 8, 128:256]
            for k, g in enumerate(groups):
                sink(g, xs, acc[k * n : k * n + n])

        def body(i, _):
            for k in range(unroll):
                part(lo + (i * unroll + k) * fuse)
            return 0

        lax.fori_loop(0, (hi - lo) // (fuse * unroll), body, 0)

    def spread_strip(v, x):
        return jnp.where(edge if v.shape[0] == 8 else edge_all[: v.shape[0]], pltpu.roll(v, (-(6 * x + R)) % 128, 1), 0.0)

    def rows_from(ref):
        return lambda x, g: ref[x, pl.ds(pl.multiple_of(g * 8, 8), 8), :]

    left = lane6 < R

    def strips_from(ref):
        n = ref.shape[1]
        return jnp.where(lane_all[:n] % 6 < R, ref[0], ref[1]), ch[0, 0:n, :], ch[1, 0:n, :]

    def band(i, j, k):
        row = stitch[pl.ds(jnp.clip(sx + i, 0, SX - 1), 1)][0, k : k + 1, :].astype(F32)
        at = lax.broadcasted_iota(jnp.int32, (1, SY), 1) == jnp.clip(sy + j, 0, SY - 1)
        return jnp.broadcast_to(jnp.sum(jnp.where(at, row, 0.0), axis=1, keepdims=True), (8, 128))

    def half(pos, width):
        return jnp.where(pos.astype(F32) < width, 0.5, 1.0).astype(F32)

    bands = {(i, j): (band(i, j, 0), band(i, j, 1)) for i in (-1, 0, 1) for j in (-1, 0, 1)}
    wrows = []
    for x in range(-R, NX + R):
        i = -1 if x < 0 else (1 if x >= NX else 0)
        row = half(jnp.full((8, 128), x - i * NX, jnp.int32), bands[i, 0][0]) * half(lane, bands[i, 0][1])
        cond = inside(i, 0)
        if cond is not None:
            row = row * jnp.where(cond, 1.0, 0.0).astype(F32)
        wrows.append(row)
    wpos = {0: lane // 6, -1: NX - R + (lane - 110) // 6, 1: (lane - 96) // 6}
    wstrips = []
    for i in (0, -1, 1):
        lane_i = (lane + 4) % 6 if i < 0 else lane6
        parts = []
        for j, pos in ((-1, NY - R + lane_i), (1, lane_i - R)):
            v = half(wpos[i], bands[i, j][0]) * half(pos, bands[i, j][1])
            parts.append(v * jnp.where(inside(i, j), 1.0, 0.0).astype(F32))
        wstrips.append(jnp.where(lane_i < R, parts[0], parts[1]))
    wstrips_at = (wstrips[0], jnp.where(lane < 110, wstrips[2], wstrips[1]), wstrips[2])

    total = psf[0]
    for j in range(1, 17):
        total = total + psf[j]

    def depth_matrix(m, k, forward):
        off = lax.broadcasted_iota(jnp.int32, (m, k), 1) - lax.broadcasted_iota(jnp.int32, (m, k), 0)
        h = jnp.zeros((m, k), F32)
        for j in range(17):
            h = jnp.where(off == j, psf[16 - j if forward else j], h)
        h = h / jnp.full((m, k), total, F32)
        hi = h.astype(BF16)
        lo = (h - hi.astype(F32)).astype(BF16)
        return jnp.concatenate([hi, hi, lo], axis=1)

    def split3(v):
        hi = v.astype(BF16)
        lo = (v - hi.astype(F32)).astype(BF16)
        return hi, lo

    nx = 3 - (sx == 0).astype(jnp.int32) - (sx == SX - 1).astype(jnp.int32)
    ny = 3 - (sy == 0).astype(jnp.int32) - (sy == SY - 1).astype(jnp.int32)
    for c in loads:
        c.wait()
    pl.semaphore_wait(barrier, nx * ny * 3 - 1)

    tcopies = [
        pltpu.make_async_remote_copy(
            src_ref=taps.at[pl.ds(s, HZ), :], dst_ref=taps.at[pl.ds(d, HZ), :],
            send_sem=t_sem.at[0, i], recv_sem=t_sem.at[1, i], device_id=device(0, 0, dz), device_id_type=MESH)
        for i, (dz, s, d) in enumerate(((1, NZ, 0), (-1, HZ, HZ + NZ)))
    ]
    e1 = copies(est1, ye1, pk.at[0], qe1, qk.at[0], HZ, DIRS, es1, er1)
    s1 = copies(spr1, ys1, pk.at[1], qs1, qk.at[1], 0, SDIRS, ss1, sr1)
    e2 = copies(est2, ye2, pk.at[2], qe2, qk.at[2], HZ, DIRS, es2, er2)
    s2 = copies(spr2, ys2, pk.at[3], qs2, qk.at[3], 0, SDIRS, ss2, sr2)

    def packed_groups(k):
        return [pk[k, 8 * g : 8 * g + 8, :] for g in range(NZ // 8)]

    each(e1, 1, "start", XS + Z_FACE)
    pack_block(est1, HZ, pk.at[0])
    pack_corners(packed_groups(0), qk.at[0])
    each(e1, 1, "start", CORN + SIDES)

    ktab[...] = jnp.zeros((8, 128), F32)
    ktab[:, 0:7] = lat_x[...]
    ktab[:, 7:14] = lat_y[...]
    for z in range(NZ):
        taps[HZ + z : HZ + z + 1, :] = ktab[pl.ds(zone[z], 1), :]
    for c in tcopies:
        c.start()

    row = lax.broadcasted_iota(jnp.int32, (256, 128), 0) % 128
    col = lax.broadcasted_iota(jnp.int32, (256, 128), 1)
    for n, pair in enumerate(PAIRS):
        for k, b in enumerate(pair):
            smat[n, :, 128 * k : 128 * k + 128] = jnp.where(row == col + (b - R), 1.0, 0.0).astype(BF16)
    lax.fori_loop(2, 10, make_taps, 0)

    def reciprocal(v):
        r = pltpu.reciprocal(v, approx=True)
        return r * (2.0 - v * r)

    def rows8(g, off=0):
        return pl.ds(pl.multiple_of(g * 8 + off, 8), 8)

    def keep_norm(g, xs, values):
        sc = scr[rows8(g), :]
        acc = jnp.zeros((8, 128), F32)
        for x, v in zip(xs, values):
            r = reciprocal(v + spread_strip(sc, x))
            rnorm[x, rows8(g), :] = r
            acc = place(acc, r, x)
        pnorm[rows8(g), :] = acc

    def keep_lest(g, xs, values):
        for x, v in zip(xs, values):
            lest[x, rows8(g), :] = v

    def keep_update(g, xs, values):
        acc = pmain[rows8(g), :]
        for x, v in zip(xs, values):
            lest[x, rows8(g), :] = v
            acc = place(acc, v, x)
        pmain[rows8(g), :] = acc

    halo_strips(*[jnp.concatenate([v] * (NZ // 8), axis=0) for v in wstrips_at], True, HZ)
    conv(lambda x, g: wrows[x], True, tuple(range(NX)), 0, NZ // 8, HZ, 1, 4, keep_norm)
    conv(rows_from(est1), False, INNER, 2, 10, 0, 2, 2, keep_lest)
    fwd1 = depth_matrix(48, 64, True)
    fwd2 = depth_matrix(32, 48, True)
    bwd = depth_matrix(64, 80, False)
    for c in tcopies:
        c.wait_recv()
    for g in (0, 1, 10, 11):
        make_taps(g, 0)

    def depth(part, spr, strip):
        blurs = []
        for a, b in part:
            pair = jnp.concatenate([lest[x] + spread_strip(scr[...], x) for x in (a, b)], axis=1)
            hi, lo = split3(pair)
            top = jnp.concatenate([hi[0:64], lo[0:64], hi[0:64]], axis=0)
            low = jnp.concatenate([hi[48:96], lo[48:96], hi[48:96]], axis=0)
            blurs.append(jnp.concatenate(
                [jnp.dot(fwd1, top, preferred_element_type=F32), jnp.dot(fwd2, low, preferred_element_type=F32)], axis=0))
        for (a, b), blur in zip(part, blurs):
            wide = jnp.concatenate([wrows[R + a][0:1], wrows[R + b][0:1]], axis=1)
            seen = jnp.concatenate([est1[R + a, 8:88, :], est1[R + b, 8:88, :]], axis=1)
            hi, lo = split3(wide * seen * reciprocal(blur))
            back = jnp.dot(bwd, jnp.concatenate([hi, lo, hi], axis=0), preferred_element_type=F32)
            for x, v in ((a, back[:, 0:128]), (b, back[:, 128:256])):
                spr[R + x] = v
                strip = [place(t, v[8 * g : 8 * g + 8], x) for g, t in enumerate(strip)]
        return strip

    for est, ye, qe, ecop, spr, ys, qs, scop, pks, last in (
        (est1, ye1, qe1, e1, spr1, ys1, qs1, s1, 1, False),
        (est2, ye2, qe2, e2, spr2, ys2, qs2, s2, 3, True),
    ):
        if last:
            conv(rows_from(est), False, INNER, 2, 10, 0, 2, 2, keep_lest)
        each(ecop, -1, "wait_recv", Z_FACE)
        conv(rows_from(est), False, INNER, 0, 2, 0, 2, 1, keep_lest)
        conv(rows_from(est), False, INNER, 10, 12, 0, 2, 1, keep_lest)
        each(ecop, -1, "wait_recv", XZ + X_LOW)
        conv(rows_from(est), False, EDGE, 0, 6, 0, 2, 3, keep_lest)
        each(ecop, -1, "wait_recv", X_HIGH)
        conv(rows_from(est), False, EDGE, 6, 12, 0, 2, 3, keep_lest)
        each(ecop, -1, "wait_recv", CORN + SIDES)
        unpack_corners(qe, HZ)
        halo_strips(*strips_from(ye), False, 0)
        strip = [jnp.zeros((8, 128), F32) for _ in range(NZ // 8)]
        strip = depth(((0, 1), (2, 13), (14, 15)), spr, strip)
        each(scop, 1, "start", X_FACE)
        pack_corners(strip, qk.at[pks])
        each(scop, 1, "start", CORN)
        strip = depth(((3, 4), (5, 6), (7, 8), (9, 10), (11, 12)), spr, strip)
        for g, t in enumerate(strip):
            pk[pks, 8 * g : 8 * g + 8, :] = t
        each(scop, 1, "start", Y_FACE)
        pmain[...] = jnp.zeros_like(pmain)
        conv(rows_from(spr), True, INNER, 0, NZ // 8, HZ, 2, 2, keep_update)
        each(scop, -1, "wait_recv", X_LOW)
        conv(rows_from(spr), True, EDGE, 0, 4, HZ, 2, 2, keep_update)
        each(scop, -1, "wait_recv", X_HIGH)
        conv(rows_from(spr), True, EDGE, 4, 8, HZ, 2, 2, keep_update)
        each(scop, -1, "wait_recv", CORN + Y_FACE)
        unpack_corners(qs, 0)
        halo_strips(*strips_from(ys), True, HZ)

        def update(x):
            return est[R + x, HZ : HZ + NZ, :] * (lest[x, 0:NZ, :] + spread_strip(scr[0:NZ, :], x)) * rnorm[x]

        if last:
            for x in range(NX):
                res[x] = update(x)
        else:
            for x in EDGE:
                est2[R + x, HZ : HZ + NZ, :] = update(x)
            each(e2, 1, "start", XS)
            pk[2] = pk[0] * (pmain[...] + scr[0:NZ, :]) * pnorm[...]
            pack_corners(packed_groups(2), qk.at[2])
            for x in INNER:
                est2[R + x, HZ : HZ + NZ, :] = update(x)
            each(e2, 1, "start", Z_FACE + CORN + SIDES)

    stores = [pltpu.make_async_copy(res.at[x], out.at[:, x, :], out_sem.at[x]) for x in range(NX)]
    for c in stores:
        c.start()
    for c in tcopies:
        c.wait_send()
    for found in (e1, s1, e2, s2):
        each(found, 1, "wait_send", XS + Z_FACE + CORN + SIDES)
    for c in stores:
        c.wait()


def body(observed, zone_of_slice, lateral_x, lateral_y, depth_psf, stitch_width):
    hbm = pl.BlockSpec(memory_space=pltpu.HBM)
    smem = pl.BlockSpec(memory_space=pltpu.SMEM)
    vmem = pl.BlockSpec(memory_space=pltpu.VMEM)
    dma = pltpu.SemaphoreType.DMA
    ne, ns = len(DIRS), len(SDIRS)
    return pl.pallas_call(
        kernel,
        out_shape=jax.ShapeDtypeStruct(observed.shape, F32),
        in_specs=[hbm, smem, vmem, vmem, smem, vmem],
        out_specs=hbm,
        scratch_shapes=[
            pltpu.VMEM((EX, EZ, NY), F32), pltpu.VMEM((EX, EZ, NY), F32),
            pltpu.VMEM((EX, NZ, NY), F32), pltpu.VMEM((EX, NZ, NY), F32),
            pltpu.VMEM((4, NZ, 128), F32), pltpu.VMEM((4, 4, 8, 128), F32),
            pltpu.VMEM((2, EZ, 128), F32), pltpu.VMEM((2, EZ, 128), F32),
            pltpu.VMEM((2, NZ, 128), F32), pltpu.VMEM((2, NZ, 128), F32),
            pltpu.VMEM((2, 2, 3, 8, 128), F32), pltpu.VMEM((2, 2, 3, 8, 128), F32),
            pltpu.VMEM((2, 2, 3, 8, 128), F32), pltpu.VMEM((2, 2, 3, 8, 128), F32),
            pltpu.VMEM((2, EZ, 128), F32),
            pltpu.VMEM((NX, EZ, NY), F32), pltpu.VMEM((NX, NZ, NY), F32), pltpu.VMEM((NX, NZ, NY), F32),
            pltpu.VMEM((8, 128), F32), pltpu.VMEM((EZ, 128), F32), pltpu.VMEM((26, EZ, 128), F32),
            pltpu.VMEM((3, 256, 256), BF16), pltpu.VMEM((EZ, 128), F32),
            pltpu.VMEM((NZ, 128), F32), pltpu.VMEM((NZ, 128), F32),
            dma((NX,)), dma((NX,)), dma((2, 2)),
            dma((ne,)), dma((ne,)), dma((ne,)), dma((ne,)),
            dma((ns,)), dma((ns,)), dma((ns,)), dma((ns,)),
        ],
        compiler_params=pltpu.CompilerParams(collective_id=0, has_side_effects=True, vmem_limit_bytes=62800 * 1024),
        name="deconvolve",
    )(observed, zone_of_slice, lateral_x, lateral_y, depth_psf, jnp.swapaxes(stitch_width, 1, 2))


def solution(mesh):
    in_specs = (P("gz", "sx", "sy"), P("gz"), P(), P(), P(), P())
    out_specs = P("gz", "sx", "sy")
    return jax.shard_map(body, mesh=mesh, in_specs=in_specs, out_specs=out_specs, check_vma=False)
```

```python
import itertools
import jax
import jax.numpy as jnp
from jax import lax
from jax.experimental import pallas as pl
from jax.experimental.pallas import tpu as pltpu
from jax.sharding import PartitionSpec as P

MESH = pl.DeviceIdType.MESH
F32 = jnp.float32
BF16 = jnp.bfloat16
NX, NY, NZ = 16, 128, 64
R = 3
HZ = 16
EZ = NZ + 2 * HZ
EX = NX + 2 * R
SX, SY, GZ = 4, 4, 8
DIRS = [d for d in itertools.product((-1, 0, 1), repeat=3) if d != (0, 0, 0)]
SDIRS = [d for d in DIRS if d[2] == 0]
KX, KY, KF, KB = 0, 7, 14, 20
EDGE = (0, 1, 2, 13, 14, 15)
INNER = tuple(range(3, 13))
PAIRS = ((0, 1), (2, 4), (5, 6))
CORNERS = {(1, 1): (78, 110), (1, -1): (81, 113), (-1, 1): (0, 96), (-1, -1): (3, 99)}


def kernel(
    obs, zone, lat_x, lat_y, psf, stitch, out,
    est1, est2, spr1, spr2, pk, qk, ye1, ye2, ys1, ys2, qe1, qe2, qs1, qs2, ch, lest, rnorm, res,
    ktab, taps, tb, smat, scr, pmain, pnorm, in_sem, out_sem, t_sem,
    es1, er1, es2, er2, ss1, sr1, ss2, sr2,
):
    sx, sy, gz = lax.axis_index("sx"), lax.axis_index("sy"), lax.axis_index("gz")
    lane = lax.broadcasted_iota(jnp.int32, (8, 128), 1)
    lane6 = lane % 6
    edge = jnp.logical_or(lane < R, lane >= NY - R)
    lane_all = lax.broadcasted_iota(jnp.int32, (EZ, 128), 1)
    edge_all = jnp.logical_or(lane_all < R, lane_all >= NY - R)

    def rows8(g, off=0):
        if isinstance(g, int):
            return slice(g * 8 + off, g * 8 + off + 8)
        return pl.ds(pl.multiple_of(g * 8 + off, 8), 8)

    loads = [pltpu.make_async_copy(obs.at[:, x, :], est1.at[R + x, pl.ds(HZ, NZ)], in_sem.at[x]) for x in range(NX)]
    for c in loads:
        c.start()

    def inside(dx, dy):
        ok = None
        for at, d, n in ((sx, dx, SX), (sy, dy, SY)):
            if d:
                t = at < n - 1 if d > 0 else at > 0
                ok = t if ok is None else jnp.logical_and(ok, t)
        return ok

    def guarded(cond, fn):
        if cond is None:
            fn()
        else:
            pl.when(cond)(fn)

    def device(dx, dy, dz):
        return (sx + dx, sy + dy, lax.rem(gz + dz + GZ, GZ))

    for dx, slot, rows in ((1, 0, 0), (-1, 1, EX - R)):
        @pl.when(jnp.logical_not(inside(-dx, 0)))
        def _(slot=slot, rows=rows):
            for e in (est1, est2, spr1, spr2):
                e[pl.ds(rows, R)] = jnp.zeros((R,) + e.shape[1:], F32)
            for q in (qe1, qe2, qs1, qs2):
                for side in range(2):
                    q[side, slot] = jnp.zeros(q.shape[2:], F32)
    for dy, side in ((1, 0), (-1, 1)):
        @pl.when(jnp.logical_not(inside(0, -dy)))
        def _(side=side):
            for y in (ye1, ye2, ys1, ys2, qe1, qe2, qs1, qs2):
                y[side] = jnp.zeros(y.shape[1:], F32)

    barrier = pltpu.get_barrier_semaphore()
    for dx, dy in itertools.product((-1, 0, 1), repeat=2):
        def greet(dx=dx, dy=dy):
            for dz in (-1, 0, 1):
                if (dx, dy, dz) != (0, 0, 0):
                    pl.semaphore_signal(barrier, inc=1, device_id=device(dx, dy, dz), device_id_type=MESH)
        guarded(inside(dx, dy), greet)

    def make_taps(g, _):
        rows = rows8(g)
        t = taps[rows, :]
        for i in range(14):
            tb[i, rows, :] = jnp.broadcast_to(t[:, i : i + 1], (8, 128))
        for k, b in enumerate((0, 1, 2, 4, 5, 6)):
            ok = {0: lane6 >= 3, 1: jnp.logical_or(lane6 == 3, lane6 == 4), 2: lane6 == 3,
                  4: lane6 == 2, 5: jnp.logical_or(lane6 == 1, lane6 == 2), 6: lane6 <= 2}[b]
            tb[KF + k, rows, :] = jnp.where(ok, jnp.broadcast_to(t[:, 7 + b : 8 + b], (8, 128)), 0.0)
            tb[KB + k, rows, :] = jnp.where(ok, jnp.broadcast_to(t[:, 13 - b : 14 - b], (8, 128)), 0.0)
        return 0


    def place(acc, v, x):
        at = jnp.logical_and(lane >= 6 * x, lane < 6 * x + 6)
        return jnp.where(at, pltpu.roll(v, 6 * x + R, 1), acc)

    def pack_block(src, off, dst):
        for g in range(NZ // 8):
            acc = jnp.zeros((8, 128), F32)
            for x in range(NX):
                acc = place(acc, src[R + x, g * 8 + off : g * 8 + off + 8, :], x)
            dst[g * 8 : g * 8 + 8, :] = acc

    def pack_corners(groups, dst):
        for k, (first, _) in enumerate(CORNERS.values()):
            acc = jnp.zeros((8, 128), F32)
            for g in range(NZ // 8):
                at = jnp.logical_and(lane >= 16 * g, lane < 16 * g + 16)
                acc = jnp.where(at, pltpu.roll(groups[g], (16 * g - first) % 128, 1), acc)
            dst[k] = acc

    def unpack_corners(src, halo):
        up = (lane + 4) % 6 < R
        for g in range((NZ + 2 * halo) // 8):
            slot, local = 1, g - halo // 8
            if local < 0:
                slot, local = 0, local + NZ // 8
            elif local >= NZ // 8:
                slot, local = 2, local - NZ // 8
            got = [pltpu.roll(src[0 if d[1] > 0 else 1, 0 if d[0] > 0 else 1, slot], (at - 16 * local) % 128, 1)
                   for d, (_, at) in CORNERS.items()]
            cu = jnp.where(up, got[0], got[1])
            cd = jnp.where(left, got[2], got[3])
            ch[0, g * 8 : g * 8 + 8, :] = jnp.where(lane < 110, cd, cu)
            ch[1, g * 8 : g * 8 + 8, :] = cd

    def copies(main, strips, packed, corners, cpacked, halo, dirs, send, recv):
        found = {}
        for i, (dx, dy, dz) in enumerate(dirs):
            zs, zd, n = {0: (0, halo, NZ), 1: (NZ - HZ, 0, HZ), -1: (0, halo + NZ, HZ)}[dz]
            if dy == 0:
                xs, xd, m = {0: (R, R, NX), 1: (NX, 0, R), -1: (R, R + NX, R)}[dx]
                src = main.at[pl.ds(xs, m), pl.ds(halo + zs, n), :]
                dst = main.at[pl.ds(xd, m), pl.ds(zd, n), :]
            elif dx == 0:
                src = packed.at[pl.ds(zs, n), :]
                dst = strips.at[0 if dy > 0 else 1, pl.ds(zd, n), :]
            else:
                src = cpacked.at[list(CORNERS).index((dx, dy))]
                dst = corners.at[0 if dy > 0 else 1, 0 if dx > 0 else 1, 1 - dz]
            found[(dx, dy, dz)] = pltpu.make_async_remote_copy(
                src_ref=src, dst_ref=dst, send_sem=send.at[i], recv_sem=recv.at[i],
                device_id=device(dx, dy, dz), device_id_type=MESH)
        return found

    X_FACE, Z_FACE, Y_FACE = [(1, 0, 0), (-1, 0, 0)], [(0, 0, 1), (0, 0, -1)], [(0, 1, 0), (0, -1, 0)]
    XZ = [(dx, 0, dz) for dx in (1, -1) for dz in (1, -1)]
    YZ = [(0, dy, dz) for dy in (1, -1) for dz in (1, -1)]
    CORN = [(dx, dy, dz) for dx in (1, -1) for dy in (1, -1) for dz in (0, 1, -1)]
    XS = XZ + X_FACE
    SIDES = [(0, dy, dz) for dy in (1, -1) for dz in (1, -1, 0)]

    def each(found, sign, what, which):
        for (dx, dy), ds in itertools.groupby([d for d in which if d in found], key=lambda d: d[:2]):
            def go(ds=tuple(ds)):
                for d in ds:
                    getattr(found[d], what)()
            guarded(inside(sign * dx, sign * dy), go)

    def taps_at(g, flip, off):
        trow = rows8(g, off)
        return ([tb[KX + (6 - a if flip else a), trow, :] for a in range(7)],
                [tb[KY + (6 - b if flip else b), trow, :] for b in range(7)])

    def halo_strips(c, c1, c2, flip, off):
        n = c.shape[0]
        rows = slice(off, off + n)
        own = lane_all[:n] < 96
        c1, c2 = jnp.where(own, c, c1), jnp.where(own, c, c2)
        al = tb[KX + 3, rows, :] * c
        for a in (0, 1, 2, 4, 5, 6):
            al = al + tb[KX + (6 - a if flip else a), rows, :] * pltpu.roll(c2 if a == 6 else c1, (18 - 6 * a) % 128, 1)
        sc = None
        for k, b in enumerate((0, 1, 2, 4, 5, 6)):
            v = tb[(KB if flip else KF) + k, rows, :] * pltpu.roll(al, (R - b) % 128, 1)
            sc = v if sc is None else sc + v
        scr[0:n, :] = sc

    def conv(rows_of, flip, xs, lo, hi, off, fuse, unroll, sink):
        def part(first):
            groups = [first + k for k in range(fuse)]
            along, taps_y = [], []
            for g in groups:
                kx, ky = taps_at(g, flip, off)
                taps_y.append(ky)
                rows = {}
                for x in xs:
                    for a in range(7):
                        if x + a not in rows:
                            rows[x + a] = rows_of(x + a, g)
                    v = kx[0] * rows[x]
                    for a in range(1, 7):
                        v = v + kx[a] * rows[x + a]
                    along.append(v)
            hi, lo_ = split3(jnp.concatenate(along, axis=0))
            both = jnp.concatenate([hi, lo_], axis=1)
            n = len(xs)
            acc = [taps_y[k // n][R] * v for k, v in enumerate(along)]
            for m, (b0, b1) in enumerate(PAIRS):
                moved = jnp.dot(both, smat[m], preferred_element_type=F32)
                for k in range(len(acc)):
                    ky = taps_y[k // n]
                    acc[k] = acc[k] + ky[b0] * moved[8 * k : 8 * k + 8, 0:128] + ky[b1] * moved[8 * k : 8 * k + 8, 128:256]
            for k, g in enumerate(groups):
                sink(g, xs, acc[k * n : k * n + n])

        def body(i, _):
            for k in range(unroll):
                part(lo + (i * unroll + k) * fuse)
            return 0

        if hi - lo == fuse * unroll:
            body(0, 0)
        else:
            lax.fori_loop(0, (hi - lo) // (fuse * unroll), body, 0)

    def spread_strip(v, x):
        return jnp.where(edge if v.shape[0] == 8 else edge_all[: v.shape[0]], pltpu.roll(v, (-(6 * x + R)) % 128, 1), 0.0)

    def rows_from(ref):
        return lambda x, g: ref[x, rows8(g), :]

    left = lane6 < R

    def strips_from(ref):
        n = ref.shape[1]
        return jnp.where(lane_all[:n] % 6 < R, ref[0], ref[1]), ch[0, 0:n, :], ch[1, 0:n, :]

    def band(i, j, k):
        row = stitch[pl.ds(jnp.clip(sx + i, 0, SX - 1), 1), pl.ds(jnp.clip(sy + j, 0, SY - 1), 1), :]
        return jnp.broadcast_to(row[0, :, k : k + 1], (8, 128))

    def half(pos, width):
        return jnp.where(pos < width, 0.5, 1.0).astype(F32)

    bands = {(i, j): (band(i, j, 0), band(i, j, 1)) for i in (-1, 0, 1) for j in (-1, 0, 1)}
    wrows = []
    for x in range(-R, NX + R):
        i = -1 if x < 0 else (1 if x >= NX else 0)
        row = half(jnp.full((8, 128), x - i * NX, jnp.int32), bands[i, 0][0]) * half(lane, bands[i, 0][1])
        cond = inside(i, 0)
        if cond is not None:
            row = row * jnp.where(cond, 1.0, 0.0).astype(F32)
        wrows.append(row)
    wpos = {0: lane // 6, -1: NX - R + (lane - 110) // 6, 1: (lane - 96) // 6}
    wstrips = []
    for i in (0, -1, 1):
        lane_i = (lane + 4) % 6 if i < 0 else lane6
        parts = []
        for j, pos in ((-1, NY - R + lane_i), (1, lane_i - R)):
            v = half(wpos[i], bands[i, j][0]) * half(pos, bands[i, j][1])
            parts.append(v * jnp.where(inside(i, j), 1.0, 0.0).astype(F32))
        wstrips.append(jnp.where(lane_i < R, parts[0], parts[1]))
    wstrips_at = (wstrips[0], jnp.where(lane < 110, wstrips[2], wstrips[1]), wstrips[2])

    total = psf[0]
    for j in range(1, 17):
        total = total + psf[j]

    def depth_matrix(m, k, forward):
        off = lax.broadcasted_iota(jnp.int32, (m, k), 1) - lax.broadcasted_iota(jnp.int32, (m, k), 0)
        h = jnp.zeros((m, k), F32)
        for j in range(17):
            h = jnp.where(off == j, psf[16 - j if forward else j], h)
        h = h / jnp.full((m, k), total, F32)
        hi = h.astype(BF16)
        lo = (h - hi.astype(F32)).astype(BF16)
        return jnp.concatenate([hi, hi, lo], axis=1)

    def split3(v):
        hi = v.astype(BF16)
        lo = (v - hi.astype(F32)).astype(BF16)
        return hi, lo

    nx = 3 - (sx == 0).astype(jnp.int32) - (sx == SX - 1).astype(jnp.int32)
    ny = 3 - (sy == 0).astype(jnp.int32) - (sy == SY - 1).astype(jnp.int32)
    for c in loads:
        c.wait()
    pl.semaphore_wait(barrier, nx * ny * 3 - 1)

    tcopies = [
        pltpu.make_async_remote_copy(
            src_ref=taps.at[pl.ds(s, HZ), :], dst_ref=taps.at[pl.ds(d, HZ), :],
            send_sem=t_sem.at[0, i], recv_sem=t_sem.at[1, i], device_id=device(0, 0, dz), device_id_type=MESH)
        for i, (dz, s, d) in enumerate(((1, NZ, 0), (-1, HZ, HZ + NZ)))
    ]
    e1 = copies(est1, ye1, pk.at[0], qe1, qk.at[0], HZ, DIRS, es1, er1)
    s1 = copies(spr1, ys1, pk.at[1], qs1, qk.at[1], 0, SDIRS, ss1, sr1)
    e2 = copies(est2, ye2, pk.at[2], qe2, qk.at[2], HZ, DIRS, es2, er2)
    s2 = copies(spr2, ys2, pk.at[3], qs2, qk.at[3], 0, SDIRS, ss2, sr2)

    def packed_groups(k):
        return [pk[k, 8 * g : 8 * g + 8, :] for g in range(NZ // 8)]

    each(e1, 1, "start", XS + Z_FACE)
    pack_block(est1, HZ, pk.at[0])
    pack_corners(packed_groups(0), qk.at[0])
    each(e1, 1, "start", CORN + SIDES)

    ktab[...] = jnp.zeros((8, 128), F32)
    ktab[:, 0:7] = lat_x[...]
    ktab[:, 7:14] = lat_y[...]
    for z in range(NZ):
        taps[HZ + z : HZ + z + 1, :] = ktab[pl.ds(zone[z], 1), :]
    for c in tcopies:
        c.start()

    row = lax.broadcasted_iota(jnp.int32, (256, 128), 0) % 128
    col = lax.broadcasted_iota(jnp.int32, (256, 128), 1)
    for n, pair in enumerate(PAIRS):
        for k, b in enumerate(pair):
            smat[n, :, 128 * k : 128 * k + 128] = jnp.where(row == col + (b - R), 1.0, 0.0).astype(BF16)
    lax.fori_loop(2, 10, make_taps, 0)

    def reciprocal(v):
        r = pltpu.reciprocal(v, approx=True)
        return r * (2.0 - v * r)

    def keep_norm(g, xs, values):
        sc = scr[rows8(g), :]
        acc = jnp.zeros((8, 128), F32)
        for x, v in zip(xs, values):
            r = reciprocal(v + spread_strip(sc, x))
            rnorm[x, rows8(g), :] = r
            acc = place(acc, r, x)
        pnorm[rows8(g), :] = acc

    def keep_lest(g, xs, values):
        for x, v in zip(xs, values):
            lest[x, rows8(g), :] = v

    def keep_update(g, xs, values):
        acc = pmain[rows8(g), :]
        for x, v in zip(xs, values):
            lest[x, rows8(g), :] = v
            acc = place(acc, v, x)
        pmain[rows8(g), :] = acc

    conv(rows_from(est1), False, INNER, 2, 10, 0, 2, 2, keep_lest)
    fwd1 = depth_matrix(48, 64, True)
    fwd2 = depth_matrix(32, 48, True)
    bwd = depth_matrix(64, 80, False)
    for c in tcopies:
        c.wait_recv()
    for g in (0, 1, 10, 11):
        make_taps(g, 0)

    def depth(part, spr, strip):
        blurs = []
        for a, b in part:
            pair = jnp.concatenate([lest[x] + spread_strip(scr[...], x) for x in (a, b)], axis=1)
            hi, lo = split3(pair)
            top = jnp.concatenate([hi[0:64], lo[0:64], hi[0:64]], axis=0)
            low = jnp.concatenate([hi[48:96], lo[48:96], hi[48:96]], axis=0)
            blurs.append(jnp.concatenate(
                [jnp.dot(fwd1, top, preferred_element_type=F32), jnp.dot(fwd2, low, preferred_element_type=F32)], axis=0))
        for (a, b), blur in zip(part, blurs):
            wide = jnp.concatenate([wrows[R + a][0:1], wrows[R + b][0:1]], axis=1)
            seen = jnp.concatenate([est1[R + a, 8:88, :], est1[R + b, 8:88, :]], axis=1)
            hi, lo = split3(wide * seen * reciprocal(blur))
            back = jnp.dot(bwd, jnp.concatenate([hi, lo, hi], axis=0), preferred_element_type=F32)
            for x, v in ((a, back[:, 0:128]), (b, back[:, 128:256])):
                spr[R + x] = v
                strip = [place(t, v[8 * g : 8 * g + 8], x) for g, t in enumerate(strip)]
        return strip

    for est, ye, qe, ecop, spr, ys, qs, scop, pks, last in (
        (est1, ye1, qe1, e1, spr1, ys1, qs1, s1, 1, False),
        (est2, ye2, qe2, e2, spr2, ys2, qs2, s2, 3, True),
    ):
        if last:
            conv(rows_from(est), False, INNER, 2, 10, 0, 2, 2, keep_lest)
        each(ecop, -1, "wait_recv", XZ + X_FACE + Z_FACE + CORN + SIDES)
        unpack_corners(qe, HZ)
        halo_strips(*strips_from(ye), False, 0)
        conv(rows_from(est), False, EDGE, 0, EZ // 8, 0, 2, 6, keep_lest)
        strip = [jnp.zeros((8, 128), F32) for _ in range(NZ // 8)]
        strip = depth(((0, 1), (2, 13), (14, 15)), spr, strip)
        each(scop, 1, "start", X_FACE)
        pack_corners(strip, qk.at[pks])
        each(scop, 1, "start", CORN)
        conv(rows_from(est), False, INNER, 0, 2, 0, 2, 1, keep_lest)
        conv(rows_from(est), False, INNER, 10, 12, 0, 2, 1, keep_lest)
        strip = depth(((3, 4), (5, 6), (7, 8), (9, 10), (11, 12)), spr, strip)
        for g, t in enumerate(strip):
            pk[pks, 8 * g : 8 * g + 8, :] = t
        each(scop, 1, "start", Y_FACE)
        pmain[...] = jnp.zeros_like(pmain)
        conv(rows_from(spr), True, INNER, 0, NZ // 8, HZ, 2, 2, keep_update)
        if not last:
            halo_strips(*[jnp.concatenate([v] * (NZ // 8), axis=0) for v in wstrips_at], True, HZ)
            conv(lambda x, g: wrows[x], True, tuple(range(NX)), 0, NZ // 8, HZ, 1, 4, keep_norm)
        each(scop, -1, "wait_recv", X_FACE + CORN + Y_FACE)
        unpack_corners(qs, 0)
        halo_strips(*strips_from(ys), True, HZ)
        conv(rows_from(spr), True, EDGE, 0, NZ // 8, HZ, 2, 4, keep_update)

        def update(x):
            return est[R + x, HZ : HZ + NZ, :] * (lest[x, 0:NZ, :] + spread_strip(scr[0:NZ, :], x)) * rnorm[x]

        if last:
            for x in range(NX):
                res[x] = update(x)
        else:
            for x in EDGE:
                est2[R + x, HZ : HZ + NZ, :] = update(x)
            each(e2, 1, "start", XS)
            pk[2] = pk[0] * (pmain[...] + scr[0:NZ, :]) * pnorm[...]
            pack_corners(packed_groups(2), qk.at[2])
            for x in INNER:
                est2[R + x, HZ : HZ + NZ, :] = update(x)
            each(e2, 1, "start", Z_FACE + CORN + SIDES)

    stores = [pltpu.make_async_copy(res.at[x], out.at[:, x, :], out_sem.at[x]) for x in range(NX)]
    for c in stores:
        c.start()
    for c in tcopies:
        c.wait_send()
    for found in (e1, s1, e2, s2):
        each(found, 1, "wait_send", XS + Z_FACE + CORN + SIDES)
    for c in stores:
        c.wait()


def body(observed, zone_of_slice, lateral_x, lateral_y, depth_psf, stitch_width):
    hbm = pl.BlockSpec(memory_space=pltpu.HBM)
    smem = pl.BlockSpec(memory_space=pltpu.SMEM)
    vmem = pl.BlockSpec(memory_space=pltpu.VMEM)
    dma = pltpu.SemaphoreType.DMA
    ne, ns = len(DIRS), len(SDIRS)
    return pl.pallas_call(
        kernel,
        out_shape=jax.ShapeDtypeStruct(observed.shape, F32),
        in_specs=[hbm, smem, vmem, vmem, smem, vmem],
        out_specs=hbm,
        scratch_shapes=[
            pltpu.VMEM((EX, EZ, NY), F32), pltpu.VMEM((EX, EZ, NY), F32),
            pltpu.VMEM((EX, NZ, NY), F32), pltpu.VMEM((EX, NZ, NY), F32),
            pltpu.VMEM((4, NZ, 128), F32), pltpu.VMEM((4, 4, 8, 128), F32),
            pltpu.VMEM((2, EZ, 128), F32), pltpu.VMEM((2, EZ, 128), F32),
            pltpu.VMEM((2, NZ, 128), F32), pltpu.VMEM((2, NZ, 128), F32),
            pltpu.VMEM((2, 2, 3, 8, 128), F32), pltpu.VMEM((2, 2, 3, 8, 128), F32),
            pltpu.VMEM((2, 2, 3, 8, 128), F32), pltpu.VMEM((2, 2, 3, 8, 128), F32),
            pltpu.VMEM((2, EZ, 128), F32),
            pltpu.VMEM((NX, EZ, NY), F32), pltpu.VMEM((NX, NZ, NY), F32), pltpu.VMEM((NX, NZ, NY), F32),
            pltpu.VMEM((8, 128), F32), pltpu.VMEM((EZ, 128), F32), pltpu.VMEM((26, EZ, 128), F32),
            pltpu.VMEM((3, 256, 256), BF16), pltpu.VMEM((EZ, 128), F32),
            pltpu.VMEM((NZ, 128), F32), pltpu.VMEM((NZ, 128), F32),
            dma((NX,)), dma((NX,)), dma((2, 2)),
            dma((ne,)), dma((ne,)), dma((ne,)), dma((ne,)),
            dma((ns,)), dma((ns,)), dma((ns,)), dma((ns,)),
        ],
        compiler_params=pltpu.CompilerParams(collective_id=0, has_side_effects=True, vmem_limit_bytes=54500 * 1024),
        name="deconvolve",
    )(observed, zone_of_slice, lateral_x, lateral_y, depth_psf, stitch_width)


def solution(mesh):
    in_specs = (P("gz", "sx", "sy"), P("gz"), P(), P(), P(), P())
    out_specs = P("gz", "sx", "sy")
    return jax.shard_map(body, mesh=mesh, in_specs=in_specs, out_specs=out_specs, check_vma=False)
```

```python
import itertools
import jax
import jax.numpy as jnp
from jax import lax
from jax.experimental import pallas as pl
from jax.experimental.pallas import tpu as pltpu
from jax.sharding import PartitionSpec as P

MESH = pl.DeviceIdType.MESH
F32 = jnp.float32
BF16 = jnp.bfloat16
NX, NY, NZ = 16, 128, 64
R = 3
HZ = 16
EZ = NZ + 2 * HZ
EX = NX + 2 * R
SX, SY, GZ = 4, 4, 8
DIRS = [d for d in itertools.product((-1, 0, 1), repeat=3) if d != (0, 0, 0)]
SDIRS = [d for d in DIRS if d[2] == 0]
KX, KY, KF, KB = 0, 7, 14, 20
EDGE = (0, 1, 2, 13, 14, 15)
INNER = tuple(range(3, 13))
PAIRS = ((0, 1), (2, 4), (5, 6))
CORNERS = {(1, 1): (78, 110), (1, -1): (81, 113), (-1, 1): (0, 96), (-1, -1): (3, 99)}


def kernel(
    obs, zone, lat_x, lat_y, psf, stitch, out,
    est1, est2, spr1, spr2, pk, qk, ye1, ye2, ys1, ys2, qe1, qe2, qs1, qs2, ch, lest, rnorm, res,
    ktab, taps, tb, smat, scr, pmain, pnorm, in_sem, out_sem, t_sem,
    es, er1, er2, ss, sr1, sr2,
):
    sx, sy, gz = lax.axis_index("sx"), lax.axis_index("sy"), lax.axis_index("gz")
    lane = lax.broadcasted_iota(jnp.int32, (8, 128), 1)
    lane6 = lane % 6
    edge = jnp.logical_or(lane < R, lane >= NY - R)
    lane_all = lax.broadcasted_iota(jnp.int32, (EZ, 128), 1)
    edge_all = jnp.logical_or(lane_all < R, lane_all >= NY - R)

    def rows8(g, off=0):
        if isinstance(g, int):
            return slice(g * 8 + off, g * 8 + off + 8)
        return pl.ds(pl.multiple_of(g * 8 + off, 8), 8)

    loads = [pltpu.make_async_copy(obs.at[:, x, :], est1.at[R + x, pl.ds(HZ, NZ)], in_sem) for x in range(NX)]
    for c in loads:
        c.start()

    def inside(dx, dy):
        ok = None
        for at, d, n in ((sx, dx, SX), (sy, dy, SY)):
            if d:
                t = at < n - 1 if d > 0 else at > 0
                ok = t if ok is None else jnp.logical_and(ok, t)
        return ok

    def guarded(cond, fn):
        if cond is None:
            fn()
        else:
            pl.when(cond)(fn)

    def device(dx, dy, dz):
        return (sx + dx, sy + dy, lax.rem(gz + dz + GZ, GZ))

    for dx, slot, rows in ((1, 0, 0), (-1, 1, EX - R)):
        @pl.when(jnp.logical_not(inside(-dx, 0)))
        def _(slot=slot, rows=rows):
            for e in (est1, est2, spr1, spr2):
                e[pl.ds(rows, R)] = jnp.zeros((R,) + e.shape[1:], F32)
            for q in (qe1, qe2, qs1, qs2):
                for side in range(2):
                    q[side, slot] = jnp.zeros(q.shape[2:], F32)
    for dy, side in ((1, 0), (-1, 1)):
        @pl.when(jnp.logical_not(inside(0, -dy)))
        def _(side=side):
            for y in (ye1, ye2, ys1, ys2, qe1, qe2, qs1, qs2):
                y[side] = jnp.zeros(y.shape[1:], F32)

    barrier = pltpu.get_barrier_semaphore()
    for dx, dy in itertools.product((-1, 0, 1), repeat=2):
        def greet(dx=dx, dy=dy):
            for dz in (-1, 0, 1):
                if (dx, dy, dz) != (0, 0, 0):
                    pl.semaphore_signal(barrier, inc=1, device_id=device(dx, dy, dz), device_id_type=MESH)
        guarded(inside(dx, dy), greet)

    def make_taps(g, _):
        rows = rows8(g)
        t = taps[rows, :]
        for i in range(14):
            tb[i, rows, :] = jnp.broadcast_to(t[:, i : i + 1], (8, 128))
        for k, b in enumerate((0, 1, 2, 4, 5, 6)):
            ok = {0: lane6 >= 3, 1: jnp.logical_or(lane6 == 3, lane6 == 4), 2: lane6 == 3,
                  4: lane6 == 2, 5: jnp.logical_or(lane6 == 1, lane6 == 2), 6: lane6 <= 2}[b]
            tb[KF + k, rows, :] = jnp.where(ok, jnp.broadcast_to(t[:, 7 + b : 8 + b], (8, 128)), 0.0)
            tb[KB + k, rows, :] = jnp.where(ok, jnp.broadcast_to(t[:, 13 - b : 14 - b], (8, 128)), 0.0)
        return 0


    def place(acc, v, x):
        at = jnp.logical_and(lane >= 6 * x, lane < 6 * x + 6)
        return jnp.where(at, pltpu.roll(v, 6 * x + R, 1), acc)

    def pack_block(src, off, dst):
        for g in range(NZ // 8):
            acc = jnp.zeros((8, 128), F32)
            for x in range(NX):
                acc = place(acc, src[R + x, g * 8 + off : g * 8 + off + 8, :], x)
            dst[g * 8 : g * 8 + 8, :] = acc

    def pack_corners(groups, dst):
        for k, (first, _) in enumerate(CORNERS.values()):
            acc = jnp.zeros((8, 128), F32)
            for g in range(NZ // 8):
                at = jnp.logical_and(lane >= 16 * g, lane < 16 * g + 16)
                acc = jnp.where(at, pltpu.roll(groups[g], (16 * g - first) % 128, 1), acc)
            dst[k] = acc

    def unpack_corners(src, halo):
        up = (lane + 4) % 6 < R
        for g in range((NZ + 2 * halo) // 8):
            slot, local = 1, g - halo // 8
            if local < 0:
                slot, local = 0, local + NZ // 8
            elif local >= NZ // 8:
                slot, local = 2, local - NZ // 8
            got = [pltpu.roll(src[0 if d[1] > 0 else 1, 0 if d[0] > 0 else 1, slot], (at - 16 * local) % 128, 1)
                   for d, (_, at) in CORNERS.items()]
            cu = jnp.where(up, got[0], got[1])
            cd = jnp.where(left, got[2], got[3])
            ch[0, g * 8 : g * 8 + 8, :] = jnp.where(lane < 110, cd, cu)
            ch[1, g * 8 : g * 8 + 8, :] = cd

    def place_of(dx, dy, dz):
        if (dx, dy) == (0, 0):
            return 8 if dz > 0 else 9
        return [d for d in itertools.product((-1, 0, 1), repeat=2) if d != (0, 0)].index((dx, dy))

    def copies(main, strips, packed, corners, cpacked, halo, dirs, send, recv):
        found = {}
        for dx, dy, dz in dirs:
            zs, zd, n = {0: (0, halo, NZ), 1: (NZ - HZ, 0, HZ), -1: (0, halo + NZ, HZ)}[dz]
            if dy == 0:
                xs, xd, m = {0: (R, R, NX), 1: (NX, 0, R), -1: (R, R + NX, R)}[dx]
                src = main.at[pl.ds(xs, m), pl.ds(halo + zs, n), :]
                dst = main.at[pl.ds(xd, m), pl.ds(zd, n), :]
            elif dx == 0:
                src = packed.at[pl.ds(zs, n), :]
                dst = strips.at[0 if dy > 0 else 1, pl.ds(zd, n), :]
            else:
                src = cpacked.at[list(CORNERS).index((dx, dy))]
                dst = corners.at[0 if dy > 0 else 1, 0 if dx > 0 else 1, 1 - dz]
            k = place_of(dx, dy, dz)
            found[(dx, dy, dz)] = pltpu.make_async_remote_copy(
                src_ref=src, dst_ref=dst, send_sem=send.at[k], recv_sem=recv.at[k],
                device_id=device(dx, dy, dz), device_id_type=MESH)
            if dz == 0:
                if dy == 0:
                    whole = main.at[pl.ds(xd, m)]
                elif dx == 0:
                    whole = strips.at[0 if dy > 0 else 1]
                elif halo:
                    whole = corners.at[0 if dy > 0 else 1, 0 if dx > 0 else 1]
                else:
                    whole = dst
                found[(dx, dy)] = pltpu.make_async_remote_copy(
                    src_ref=whole, dst_ref=whole, send_sem=send.at[k], recv_sem=recv.at[k],
                    device_id=device(dx, dy, 0), device_id_type=MESH)
        return found

    X_FACE, Z_FACE, Y_FACE = [(1, 0, 0), (-1, 0, 0)], [(0, 0, 1), (0, 0, -1)], [(0, 1, 0), (0, -1, 0)]
    XZ = [(dx, 0, dz) for dx in (1, -1) for dz in (1, -1)]
    YZ = [(0, dy, dz) for dy in (1, -1) for dz in (1, -1)]
    CORN = [(dx, dy, dz) for dx in (1, -1) for dy in (1, -1) for dz in (0, 1, -1)]
    XS = XZ + X_FACE
    WAITS = X_FACE + [d for d in CORN if d[2] == 0] + Y_FACE + Z_FACE
    SIDES = [(0, dy, dz) for dy in (1, -1) for dz in (1, -1, 0)]

    def each(found, sign, what, which):
        for (dx, dy), ds in itertools.groupby([d for d in which if d in found], key=lambda d: d[:2]):
            def go(ds=tuple(ds), dx=dx, dy=dy):
                if what != "start" and (dx, dy) in found:
                    ds = [(dx, dy)]
                for d in ds:
                    getattr(found[d], what)()
            guarded(inside(sign * dx, sign * dy), go)

    def taps_at(g, flip, off):
        trow = rows8(g, off)
        return ([tb[KX + (6 - a if flip else a), trow, :] for a in range(7)],
                [tb[KY + (6 - b if flip else b), trow, :] for b in range(7)])

    def halo_strips(c, c1, c2, flip, off):
        n = c.shape[0]
        rows = slice(off, off + n)
        own = lane_all[:n] < 96
        c1, c2 = jnp.where(own, c, c1), jnp.where(own, c, c2)
        al = tb[KX + 3, rows, :] * c
        for a in (0, 1, 2, 4, 5, 6):
            al = al + tb[KX + (6 - a if flip else a), rows, :] * pltpu.roll(c2 if a == 6 else c1, (18 - 6 * a) % 128, 1)
        sc = None
        for k, b in enumerate((0, 1, 2, 4, 5, 6)):
            v = tb[(KB if flip else KF) + k, rows, :] * pltpu.roll(al, (R - b) % 128, 1)
            sc = v if sc is None else sc + v
        scr[0:n, :] = sc

    def conv(rows_of, flip, xs, lo, hi, off, fuse, unroll, sink):
        def part(first):
            groups = [first + k for k in range(fuse)]
            along, taps_y = [], []
            for g in groups:
                kx, ky = taps_at(g, flip, off)
                taps_y.append(ky)
                rows = {}
                for x in xs:
                    for a in range(7):
                        if x + a not in rows:
                            rows[x + a] = rows_of(x + a, g)
                    v = kx[0] * rows[x]
                    for a in range(1, 7):
                        v = v + kx[a] * rows[x + a]
                    along.append(v)
            hi, lo_ = split3(jnp.concatenate(along, axis=0))
            both = jnp.concatenate([hi, lo_], axis=1)
            n = len(xs)
            acc = [taps_y[k // n][R] * v for k, v in enumerate(along)]
            for m, (b0, b1) in enumerate(PAIRS):
                moved = jnp.dot(both, smat[m], preferred_element_type=F32)
                for k in range(len(acc)):
                    ky = taps_y[k // n]
                    acc[k] = acc[k] + ky[b0] * moved[8 * k : 8 * k + 8, 0:128] + ky[b1] * moved[8 * k : 8 * k + 8, 128:256]
            for k, g in enumerate(groups):
                sink(g, xs, acc[k * n : k * n + n])

        def body(i, _):
            for k in range(unroll):
                part(lo + (i * unroll + k) * fuse)
            return 0

        if hi - lo == fuse * unroll:
            body(0, 0)
        else:
            lax.fori_loop(0, (hi - lo) // (fuse * unroll), body, 0)

    def spread_strip(v, x):
        return jnp.where(edge if v.shape[0] == 8 else edge_all[: v.shape[0]], pltpu.roll(v, (-(6 * x + R)) % 128, 1), 0.0)

    def rows_from(ref):
        return lambda x, g: ref[x, rows8(g), :]

    left = lane6 < R

    def strips_from(ref):
        n = ref.shape[1]
        return jnp.where(lane_all[:n] % 6 < R, ref[0], ref[1]), ch[0, 0:n, :], ch[1, 0:n, :]

    def band(i, j, k):
        row = stitch[pl.ds(jnp.clip(sx + i, 0, SX - 1), 1), pl.ds(jnp.clip(sy + j, 0, SY - 1), 1), :]
        return jnp.broadcast_to(row[0, :, k : k + 1], (8, 128))

    def half(pos, width):
        return jnp.where(pos < width, 0.5, 1.0).astype(F32)

    bands = {(i, j): (band(i, j, 0), band(i, j, 1)) for i in (-1, 0, 1) for j in (-1, 0, 1)}
    wrows = []
    for x in range(-R, NX + R):
        i = -1 if x < 0 else (1 if x >= NX else 0)
        row = half(jnp.full((8, 128), x - i * NX, jnp.int32), bands[i, 0][0]) * half(lane, bands[i, 0][1])
        cond = inside(i, 0)
        if cond is not None:
            row = row * jnp.where(cond, 1.0, 0.0).astype(F32)
        wrows.append(row)
    wpos = {0: lane // 6, -1: NX - R + (lane - 110) // 6, 1: (lane - 96) // 6}
    wstrips = []
    for i in (0, -1, 1):
        lane_i = (lane + 4) % 6 if i < 0 else lane6
        parts = []
        for j, pos in ((-1, NY - R + lane_i), (1, lane_i - R)):
            v = half(wpos[i], bands[i, j][0]) * half(pos, bands[i, j][1])
            parts.append(v * jnp.where(inside(i, j), 1.0, 0.0).astype(F32))
        wstrips.append(jnp.where(lane_i < R, parts[0], parts[1]))
    wstrips_at = (wstrips[0], jnp.where(lane < 110, wstrips[2], wstrips[1]), wstrips[2])

    total = psf[0]
    for j in range(1, 17):
        total = total + psf[j]

    def depth_matrix(m, k, forward):
        off = lax.broadcasted_iota(jnp.int32, (m, k), 1) - lax.broadcasted_iota(jnp.int32, (m, k), 0)
        h = jnp.zeros((m, k), F32)
        for j in range(17):
            h = jnp.where(off == j, psf[16 - j if forward else j], h)
        h = h / jnp.full((m, k), total, F32)
        hi = h.astype(BF16)
        lo = (h - hi.astype(F32)).astype(BF16)
        return jnp.concatenate([hi, hi, lo], axis=1)

    def split3(v):
        hi = v.astype(BF16)
        lo = (v - hi.astype(F32)).astype(BF16)
        return hi, lo

    nx = 3 - (sx == 0).astype(jnp.int32) - (sx == SX - 1).astype(jnp.int32)
    ny = 3 - (sy == 0).astype(jnp.int32) - (sy == SY - 1).astype(jnp.int32)
    mine = est1.at[pl.ds(R, NX), pl.ds(HZ, NZ)]
    pltpu.make_async_copy(mine, mine, in_sem).wait()
    pl.semaphore_wait(barrier, nx * ny * 3 - 1)

    tcopies = [
        pltpu.make_async_remote_copy(
            src_ref=taps.at[pl.ds(s, HZ), :], dst_ref=taps.at[pl.ds(d, HZ), :],
            send_sem=t_sem.at[0, i], recv_sem=t_sem.at[1, i], device_id=device(0, 0, dz), device_id_type=MESH)
        for i, (dz, s, d) in enumerate(((1, NZ, 0), (-1, HZ, HZ + NZ)))
    ]
    e1 = copies(est1, ye1, pk.at[0], qe1, qk.at[0], HZ, DIRS, es, er1)
    s1 = copies(spr1, ys1, pk.at[1], qs1, qk.at[1], 0, SDIRS, ss, sr1)
    e2 = copies(est2, ye2, pk.at[2], qe2, qk.at[2], HZ, DIRS, es, er2)
    s2 = copies(spr2, ys2, pk.at[3], qs2, qk.at[3], 0, SDIRS, ss, sr2)

    def packed_groups(k):
        return [pk[k, 8 * g : 8 * g + 8, :] for g in range(NZ // 8)]

    each(e1, 1, "start", XS + Z_FACE)
    pack_block(est1, HZ, pk.at[0])
    pack_corners(packed_groups(0), qk.at[0])
    each(e1, 1, "start", CORN + SIDES)

    ktab[...] = jnp.zeros((8, 128), F32)
    ktab[:, 0:7] = lat_x[...]
    ktab[:, 7:14] = lat_y[...]
    for z in range(NZ):
        taps[HZ + z : HZ + z + 1, :] = ktab[pl.ds(zone[z], 1), :]
    for c in tcopies:
        c.start()

    row = lax.broadcasted_iota(jnp.int32, (256, 128), 0) % 128
    col = lax.broadcasted_iota(jnp.int32, (256, 128), 1)
    for n, pair in enumerate(PAIRS):
        for k, b in enumerate(pair):
            smat[n, :, 128 * k : 128 * k + 128] = jnp.where(row == col + (b - R), 1.0, 0.0).astype(BF16)
    lax.fori_loop(2, 10, make_taps, 0)

    def reciprocal(v):
        r = pltpu.reciprocal(v, approx=True)
        return r * (2.0 - v * r)

    def keep_norm(g, xs, values):
        sc = scr[rows8(g), :]
        acc = jnp.zeros((8, 128), F32)
        for x, v in zip(xs, values):
            r = reciprocal(v + spread_strip(sc, x))
            rnorm[x, rows8(g), :] = r
            acc = place(acc, r, x)
        pnorm[rows8(g), :] = acc

    def keep_lest(g, xs, values):
        for x, v in zip(xs, values):
            lest[x, rows8(g), :] = v

    def keep_update(g, xs, values):
        acc = pmain[rows8(g), :]
        for x, v in zip(xs, values):
            lest[x, rows8(g), :] = v
            acc = place(acc, v, x)
        pmain[rows8(g), :] = acc

    conv(rows_from(est1), False, INNER, 2, 10, 0, 2, 2, keep_lest)
    fwd1 = depth_matrix(48, 64, True)
    fwd2 = depth_matrix(32, 48, True)
    bwd = depth_matrix(64, 80, False)
    for c in tcopies:
        c.wait_recv()
    for g in (0, 1, 10, 11):
        make_taps(g, 0)

    def depth(part, spr, strip):
        blurs = []
        for a, b in part:
            pair = jnp.concatenate([lest[x] + spread_strip(scr[...], x) for x in (a, b)], axis=1)
            hi, lo = split3(pair)
            top = jnp.concatenate([hi[0:64], lo[0:64], hi[0:64]], axis=0)
            low = jnp.concatenate([hi[48:96], lo[48:96], hi[48:96]], axis=0)
            blurs.append(jnp.concatenate(
                [jnp.dot(fwd1, top, preferred_element_type=F32), jnp.dot(fwd2, low, preferred_element_type=F32)], axis=0))
        for (a, b), blur in zip(part, blurs):
            wide = jnp.concatenate([wrows[R + a][0:1], wrows[R + b][0:1]], axis=1)
            seen = jnp.concatenate([est1[R + a, 8:88, :], est1[R + b, 8:88, :]], axis=1)
            hi, lo = split3(wide * seen * reciprocal(blur))
            back = jnp.dot(bwd, jnp.concatenate([hi, lo, hi], axis=0), preferred_element_type=F32)
            for x, v in ((a, back[:, 0:128]), (b, back[:, 128:256])):
                spr[R + x] = v
                strip = [place(t, v[8 * g : 8 * g + 8], x) for g, t in enumerate(strip)]
        return strip

    for est, ye, qe, ecop, spr, ys, qs, scop, pks, last in (
        (est1, ye1, qe1, e1, spr1, ys1, qs1, s1, 1, False),
        (est2, ye2, qe2, e2, spr2, ys2, qs2, s2, 3, True),
    ):
        if last:
            conv(rows_from(est), False, INNER, 2, 10, 0, 2, 2, keep_lest)
        each(ecop, -1, "wait_recv", WAITS)
        unpack_corners(qe, HZ)
        halo_strips(*strips_from(ye), False, 0)
        conv(rows_from(est), False, EDGE, 0, EZ // 8, 0, 2, 6, keep_lest)
        strip = [jnp.zeros((8, 128), F32) for _ in range(NZ // 8)]
        strip = depth(((0, 1), (2, 13), (14, 15)), spr, strip)
        if last:
            each(s1, 1, "wait_send", WAITS)
        each(scop, 1, "start", X_FACE)
        pack_corners(strip, qk.at[pks])
        each(scop, 1, "start", CORN)
        conv(rows_from(est), False, INNER, 0, 2, 0, 2, 1, keep_lest)
        conv(rows_from(est), False, INNER, 10, 12, 0, 2, 1, keep_lest)
        strip = depth(((3, 4), (5, 6), (7, 8), (9, 10), (11, 12)), spr, strip)
        for g, t in enumerate(strip):
            pk[pks, 8 * g : 8 * g + 8, :] = t
        each(scop, 1, "start", Y_FACE)
        pmain[...] = jnp.zeros_like(pmain)
        conv(rows_from(spr), True, INNER, 0, NZ // 8, HZ, 2, 2, keep_update)
        if not last:
            halo_strips(*[jnp.concatenate([v] * (NZ // 8), axis=0) for v in wstrips_at], True, HZ)
            conv(lambda x, g: wrows[x], True, tuple(range(NX)), 0, NZ // 8, HZ, 1, 4, keep_norm)
        each(scop, -1, "wait_recv", WAITS)
        unpack_corners(qs, 0)
        halo_strips(*strips_from(ys), True, HZ)
        conv(rows_from(spr), True, EDGE, 0, NZ // 8, HZ, 2, 4, keep_update)

        def update(x):
            return est[R + x, HZ : HZ + NZ, :] * (lest[x, 0:NZ, :] + spread_strip(scr[0:NZ, :], x)) * rnorm[x]

        if last:
            for x in range(NX):
                res[x] = update(x)
        else:
            for x in EDGE:
                est2[R + x, HZ : HZ + NZ, :] = update(x)
            each(e1, 1, "wait_send", WAITS)
            each(e2, 1, "start", XS)
            pk[2] = pk[0] * (pmain[...] + scr[0:NZ, :]) * pnorm[...]
            pack_corners(packed_groups(2), qk.at[2])
            for x in INNER:
                est2[R + x, HZ : HZ + NZ, :] = update(x)
            each(e2, 1, "start", Z_FACE + CORN + SIDES)

    stores = [pltpu.make_async_copy(res.at[x], out.at[:, x, :], out_sem) for x in range(NX)]
    for c in stores:
        c.start()
    for c in tcopies:
        c.wait_send()
    for found in (e2, s2):
        each(found, 1, "wait_send", WAITS)
    pltpu.make_async_copy(res, res, out_sem).wait()


def body(observed, zone_of_slice, lateral_x, lateral_y, depth_psf, stitch_width):
    hbm = pl.BlockSpec(memory_space=pltpu.HBM)
    smem = pl.BlockSpec(memory_space=pltpu.SMEM)
    vmem = pl.BlockSpec(memory_space=pltpu.VMEM)
    dma = pltpu.SemaphoreType.DMA
    return pl.pallas_call(
        kernel,
        out_shape=jax.ShapeDtypeStruct(observed.shape, F32),
        in_specs=[hbm, smem, vmem, vmem, smem, vmem],
        out_specs=hbm,
        scratch_shapes=[
            pltpu.VMEM((EX, EZ, NY), F32), pltpu.VMEM((EX, EZ, NY), F32),
            pltpu.VMEM((EX, NZ, NY), F32), pltpu.VMEM((EX, NZ, NY), F32),
            pltpu.VMEM((4, NZ, 128), F32), pltpu.VMEM((4, 4, 8, 128), F32),
            pltpu.VMEM((2, EZ, 128), F32), pltpu.VMEM((2, EZ, 128), F32),
            pltpu.VMEM((2, NZ, 128), F32), pltpu.VMEM((2, NZ, 128), F32),
            pltpu.VMEM((2, 2, 3, 8, 128), F32), pltpu.VMEM((2, 2, 3, 8, 128), F32),
            pltpu.VMEM((2, 2, 3, 8, 128), F32), pltpu.VMEM((2, 2, 3, 8, 128), F32),
            pltpu.VMEM((2, EZ, 128), F32),
            pltpu.VMEM((NX, EZ, NY), F32), pltpu.VMEM((NX, NZ, NY), F32), pltpu.VMEM((NX, NZ, NY), F32),
            pltpu.VMEM((8, 128), F32), pltpu.VMEM((EZ, 128), F32), pltpu.VMEM((26, EZ, 128), F32),
            pltpu.VMEM((3, 256, 256), BF16), pltpu.VMEM((EZ, 128), F32),
            pltpu.VMEM((NZ, 128), F32), pltpu.VMEM((NZ, 128), F32),
            dma(()), dma(()), dma((2, 2)),
            dma((10,)), dma((10,)), dma((10,)), dma((8,)), dma((8,)), dma((8,)),
        ],
        compiler_params=pltpu.CompilerParams(collective_id=0, has_side_effects=True, vmem_limit_bytes=54500 * 1024),
        name="deconvolve",
    )(observed, zone_of_slice, lateral_x, lateral_y, depth_psf, stitch_width)


def solution(mesh):
    in_specs = (P("gz", "sx", "sy"), P("gz"), P(), P(), P(), P())
    out_specs = P("gz", "sx", "sy")
    return jax.shard_map(body, mesh=mesh, in_specs=in_specs, out_specs=out_specs, check_vma=False)
```

```python
import itertools
import jax
import jax.numpy as jnp
from jax import lax
from jax.experimental import pallas as pl
from jax.experimental.pallas import tpu as pltpu
from jax.sharding import PartitionSpec as P

MESH = pl.DeviceIdType.MESH
F32 = jnp.float32
BF16 = jnp.bfloat16
NX, NY, NZ = 16, 128, 64
R = 3
HZ = 16
EZ = NZ + 2 * HZ
EX = NX + 2 * R
SX, SY, GZ = 4, 4, 8
DIRS = [d for d in itertools.product((-1, 0, 1), repeat=3) if d != (0, 0, 0)]
SDIRS = [d for d in DIRS if d[2] == 0]
KX, KY, KF, KB = 0, 7, 14, 20
EDGE = (0, 1, 2, 13, 14, 15)
INNER = tuple(range(3, 13))
PAIRS = ((0, 1), (2, 4), (5, 6))
CORNERS = {(1, 1): (78, 110), (1, -1): (81, 113), (-1, 1): (0, 96), (-1, -1): (3, 99)}


def kernel(
    obs, zone_in, lat_x_in, lat_y_in, psf_in, stitch_in, out,
    zone, lat_x, lat_y, psf, stitch, small_sem,
    est1, est2, spr1, spr2, pk, qk, ye1, ye2, ys1, ys2, qe1, qe2, qs1, qs2, ch, lest, rnorm, res,
    ktab, taps, tb, smat, scr, pmain, pnorm, in_sem, out_sem, t_sem,
    es, er1, er2, ss, sr1, sr2,
):
    sx, sy, gz = lax.axis_index("sx"), lax.axis_index("sy"), lax.axis_index("gz")
    lane = lax.broadcasted_iota(jnp.int32, (8, 128), 1)
    lane6 = lane % 6
    edge = jnp.logical_or(lane < R, lane >= NY - R)
    lane_all = lax.broadcasted_iota(jnp.int32, (EZ, 128), 1)
    edge_all = jnp.logical_or(lane_all < R, lane_all >= NY - R)

    def rows8(g, off=0):
        if isinstance(g, int):
            return slice(g * 8 + off, g * 8 + off + 8)
        return pl.ds(pl.multiple_of(g * 8 + off, 8), 8)

    loads = [pltpu.make_async_copy(obs.at[:, x, :], est1.at[R + x, pl.ds(HZ, NZ)], in_sem) for x in range(NX)]
    smalls = [
        pltpu.make_async_copy(a, b, small_sem.at[i])
        for i, (a, b) in enumerate(((zone_in, zone), (lat_x_in, lat_x), (lat_y_in, lat_y), (psf_in, psf), (stitch_in, stitch)))
    ]
    for c in loads + smalls:
        c.start()

    def inside(dx, dy):
        ok = None
        for at, d, n in ((sx, dx, SX), (sy, dy, SY)):
            if d:
                t = at < n - 1 if d > 0 else at > 0
                ok = t if ok is None else jnp.logical_and(ok, t)
        return ok

    def guarded(cond, fn):
        if cond is None:
            fn()
        else:
            pl.when(cond)(fn)

    def device(dx, dy, dz):
        return (sx + dx, sy + dy, lax.rem(gz + dz + GZ, GZ))

    for dx, slot, rows in ((1, 0, 0), (-1, 1, EX - R)):
        @pl.when(jnp.logical_not(inside(-dx, 0)))
        def _(slot=slot, rows=rows):
            for e in (est1, est2, spr1, spr2):
                e[pl.ds(rows, R)] = jnp.zeros((R,) + e.shape[1:], F32)
            for q in (qe1, qe2, qs1, qs2):
                for side in range(2):
                    q[side, slot] = jnp.zeros(q.shape[2:], F32)
    for dy, side in ((1, 0), (-1, 1)):
        @pl.when(jnp.logical_not(inside(0, -dy)))
        def _(side=side):
            for y in (ye1, ye2, ys1, ys2, qe1, qe2, qs1, qs2):
                y[side] = jnp.zeros(y.shape[1:], F32)

    barrier = pltpu.get_barrier_semaphore()
    for dx, dy in itertools.product((-1, 0, 1), repeat=2):
        def greet(dx=dx, dy=dy):
            for dz in (-1, 0, 1):
                if (dx, dy, dz) != (0, 0, 0):
                    pl.semaphore_signal(barrier, inc=1, device_id=device(dx, dy, dz), device_id_type=MESH)
        guarded(inside(dx, dy), greet)

    def make_taps(g, _):
        rows = rows8(g)
        t = taps[rows, :]
        for i in range(14):
            tb[i, rows, :] = jnp.broadcast_to(t[:, i : i + 1], (8, 128))
        for k, b in enumerate((0, 1, 2, 4, 5, 6)):
            ok = {0: lane6 >= 3, 1: jnp.logical_or(lane6 == 3, lane6 == 4), 2: lane6 == 3,
                  4: lane6 == 2, 5: jnp.logical_or(lane6 == 1, lane6 == 2), 6: lane6 <= 2}[b]
            tb[KF + k, rows, :] = jnp.where(ok, jnp.broadcast_to(t[:, 7 + b : 8 + b], (8, 128)), 0.0)
            tb[KB + k, rows, :] = jnp.where(ok, jnp.broadcast_to(t[:, 13 - b : 14 - b], (8, 128)), 0.0)
        return 0


    def place(acc, v, x):
        at = jnp.logical_and(lane >= 6 * x, lane < 6 * x + 6)
        return jnp.where(at, pltpu.roll(v, 6 * x + R, 1), acc)

    def pack_block(src, off, dst):
        for g in range(NZ // 8):
            acc = jnp.zeros((8, 128), F32)
            for x in range(NX):
                acc = place(acc, src[R + x, g * 8 + off : g * 8 + off + 8, :], x)
            dst[g * 8 : g * 8 + 8, :] = acc

    def pack_corners(groups, dst):
        for k, (first, _) in enumerate(CORNERS.values()):
            acc = jnp.zeros((8, 128), F32)
            for g in range(NZ // 8):
                at = jnp.logical_and(lane >= 16 * g, lane < 16 * g + 16)
                acc = jnp.where(at, pltpu.roll(groups[g], (16 * g - first) % 128, 1), acc)
            dst[k] = acc

    def unpack_corners(src, halo):
        up = (lane + 4) % 6 < R
        for g in range((NZ + 2 * halo) // 8):
            slot, local = 1, g - halo // 8
            if local < 0:
                slot, local = 0, local + NZ // 8
            elif local >= NZ // 8:
                slot, local = 2, local - NZ // 8
            got = [pltpu.roll(src[0 if d[1] > 0 else 1, 0 if d[0] > 0 else 1, slot], (at - 16 * local) % 128, 1)
                   for d, (_, at) in CORNERS.items()]
            cu = jnp.where(up, got[0], got[1])
            cd = jnp.where(left, got[2], got[3])
            ch[0, g * 8 : g * 8 + 8, :] = jnp.where(lane < 110, cd, cu)
            ch[1, g * 8 : g * 8 + 8, :] = cd

    def place_of(dx, dy, dz):
        if (dx, dy) == (0, 0):
            return 8 if dz > 0 else 9
        return [d for d in itertools.product((-1, 0, 1), repeat=2) if d != (0, 0)].index((dx, dy))

    def copies(main, strips, packed, corners, cpacked, halo, dirs, send, recv):
        found = {}
        for dx, dy, dz in dirs:
            zs, zd, n = {0: (0, halo, NZ), 1: (NZ - HZ, 0, HZ), -1: (0, halo + NZ, HZ)}[dz]
            if dy == 0:
                xs, xd, m = {0: (R, R, NX), 1: (NX, 0, R), -1: (R, R + NX, R)}[dx]
                src = main.at[pl.ds(xs, m), pl.ds(halo + zs, n), :]
                dst = main.at[pl.ds(xd, m), pl.ds(zd, n), :]
            elif dx == 0:
                src = packed.at[pl.ds(zs, n), :]
                dst = strips.at[0 if dy > 0 else 1, pl.ds(zd, n), :]
            else:
                src = cpacked.at[list(CORNERS).index((dx, dy))]
                dst = corners.at[0 if dy > 0 else 1, 0 if dx > 0 else 1, 1 - dz]
            k = place_of(dx, dy, dz)
            found[(dx, dy, dz)] = pltpu.make_async_remote_copy(
                src_ref=src, dst_ref=dst, send_sem=send.at[k], recv_sem=recv.at[k],
                device_id=device(dx, dy, dz), device_id_type=MESH)
            if dz == 0:
                if dy == 0:
                    whole = main.at[pl.ds(xd, m)]
                elif dx == 0:
                    whole = strips.at[0 if dy > 0 else 1]
                elif halo:
                    whole = corners.at[0 if dy > 0 else 1, 0 if dx > 0 else 1]
                else:
                    whole = dst
                found[(dx, dy)] = pltpu.make_async_remote_copy(
                    src_ref=whole, dst_ref=whole, send_sem=send.at[k], recv_sem=recv.at[k],
                    device_id=device(dx, dy, 0), device_id_type=MESH)
        return found

    X_FACE, Z_FACE, Y_FACE = [(1, 0, 0), (-1, 0, 0)], [(0, 0, 1), (0, 0, -1)], [(0, 1, 0), (0, -1, 0)]
    XZ = [(dx, 0, dz) for dx in (1, -1) for dz in (1, -1)]
    YZ = [(0, dy, dz) for dy in (1, -1) for dz in (1, -1)]
    CORN = [(dx, dy, dz) for dx in (1, -1) for dy in (1, -1) for dz in (0, 1, -1)]
    XS = XZ + X_FACE
    WAITS = X_FACE + [d for d in CORN if d[2] == 0] + Y_FACE + Z_FACE
    SIDES = [(0, dy, dz) for dy in (1, -1) for dz in (1, -1, 0)]

    def each(found, sign, what, which):
        for (dx, dy), ds in itertools.groupby([d for d in which if d in found], key=lambda d: d[:2]):
            def go(ds=tuple(ds), dx=dx, dy=dy):
                if what != "start" and (dx, dy) in found:
                    ds = [(dx, dy)]
                for d in ds:
                    getattr(found[d], what)()
            guarded(inside(sign * dx, sign * dy), go)

    def taps_at(g, flip, off):
        trow = rows8(g, off)
        return ([tb[KX + (6 - a if flip else a), trow, :] for a in range(7)],
                [tb[KY + (6 - b if flip else b), trow, :] for b in range(7)])

    def halo_strips(c, c1, c2, flip, off):
        n = c.shape[0]
        rows = slice(off, off + n)
        own = lane_all[:n] < 96
        c1, c2 = jnp.where(own, c, c1), jnp.where(own, c, c2)
        al = tb[KX + 3, rows, :] * c
        for a in (0, 1, 2, 4, 5, 6):
            al = al + tb[KX + (6 - a if flip else a), rows, :] * pltpu.roll(c2 if a == 6 else c1, (18 - 6 * a) % 128, 1)
        sc = None
        for k, b in enumerate((0, 1, 2, 4, 5, 6)):
            v = tb[(KB if flip else KF) + k, rows, :] * pltpu.roll(al, (R - b) % 128, 1)
            sc = v if sc is None else sc + v
        scr[0:n, :] = sc

    def conv(rows_of, flip, xs, lo, hi, off, fuse, unroll, sink):
        def part(first):
            groups = [first + k for k in range(fuse)]
            along, taps_y = [], []
            for g in groups:
                kx, ky = taps_at(g, flip, off)
                taps_y.append(ky)
                rows = {}
                for x in xs:
                    for a in range(7):
                        if x + a not in rows:
                            rows[x + a] = rows_of(x + a, g)
                    v = kx[0] * rows[x]
                    for a in range(1, 7):
                        v = v + kx[a] * rows[x + a]
                    along.append(v)
            hi, lo_ = split3(jnp.concatenate(along, axis=0))
            both = jnp.concatenate([hi, lo_], axis=1)
            n = len(xs)
            acc = [taps_y[k // n][R] * v for k, v in enumerate(along)]
            for m, (b0, b1) in enumerate(PAIRS):
                moved = jnp.dot(both, smat[m], preferred_element_type=F32)
                for k in range(len(acc)):
                    ky = taps_y[k // n]
                    acc[k] = acc[k] + ky[b0] * moved[8 * k : 8 * k + 8, 0:128] + ky[b1] * moved[8 * k : 8 * k + 8, 128:256]
            for k, g in enumerate(groups):
                sink(g, xs, acc[k * n : k * n + n])

        def body(i, _):
            for k in range(unroll):
                part(lo + (i * unroll + k) * fuse)
            return 0

        if hi - lo == fuse * unroll:
            body(0, 0)
        else:
            lax.fori_loop(0, (hi - lo) // (fuse * unroll), body, 0)

    def spread_strip(v, x):
        return jnp.where(edge if v.shape[0] == 8 else edge_all[: v.shape[0]], pltpu.roll(v, (-(6 * x + R)) % 128, 1), 0.0)

    def rows_from(ref):
        return lambda x, g: ref[x, rows8(g), :]

    left = lane6 < R

    def strips_from(ref):
        n = ref.shape[1]
        return jnp.where(lane_all[:n] % 6 < R, ref[0], ref[1]), ch[0, 0:n, :], ch[1, 0:n, :]

    def depth_matrix(m, k, forward):
        off = lax.broadcasted_iota(jnp.int32, (m, k), 1) - lax.broadcasted_iota(jnp.int32, (m, k), 0)
        h = jnp.zeros((m, k), F32)
        for j in range(17):
            h = jnp.where(off == j, psf[16 - j if forward else j], h)
        h = h / jnp.full((m, k), total, F32)
        hi = h.astype(BF16)
        lo = (h - hi.astype(F32)).astype(BF16)
        return jnp.concatenate([hi, hi, lo], axis=1)

    def split3(v):
        hi = v.astype(BF16)
        lo = (v - hi.astype(F32)).astype(BF16)
        return hi, lo

    nx = 3 - (sx == 0).astype(jnp.int32) - (sx == SX - 1).astype(jnp.int32)
    ny = 3 - (sy == 0).astype(jnp.int32) - (sy == SY - 1).astype(jnp.int32)
    for c in smalls:
        c.wait()
    mine = est1.at[pl.ds(R, NX), pl.ds(HZ, NZ)]
    pltpu.make_async_copy(mine, mine, in_sem).wait()
    pl.semaphore_wait(barrier, nx * ny * 3 - 1)

    tcopies = [
        pltpu.make_async_remote_copy(
            src_ref=taps.at[pl.ds(s, HZ), :], dst_ref=taps.at[pl.ds(d, HZ), :],
            send_sem=t_sem.at[0, i], recv_sem=t_sem.at[1, i], device_id=device(0, 0, dz), device_id_type=MESH)
        for i, (dz, s, d) in enumerate(((1, NZ, 0), (-1, HZ, HZ + NZ)))
    ]
    e1 = copies(est1, ye1, pk.at[0], qe1, qk.at[0], HZ, DIRS, es, er1)
    s1 = copies(spr1, ys1, pk.at[1], qs1, qk.at[1], 0, SDIRS, ss, sr1)
    e2 = copies(est2, ye2, pk.at[2], qe2, qk.at[2], HZ, DIRS, es, er2)
    s2 = copies(spr2, ys2, pk.at[3], qs2, qk.at[3], 0, SDIRS, ss, sr2)

    def packed_groups(k):
        return [pk[k, 8 * g : 8 * g + 8, :] for g in range(NZ // 8)]

    each(e1, 1, "start", XS + Z_FACE)
    pack_block(est1, HZ, pk.at[0])
    pack_corners(packed_groups(0), qk.at[0])
    each(e1, 1, "start", CORN + SIDES)

    ktab[...] = jnp.zeros((8, 128), F32)
    ktab[:, 0:7] = lat_x[...]
    ktab[:, 7:14] = lat_y[...]
    for z in range(NZ):
        taps[HZ + z : HZ + z + 1, :] = ktab[pl.ds(zone[z], 1), :]
    for c in tcopies:
        c.start()

    def band(i, j, k):
        row = stitch[pl.ds(jnp.clip(sx + i, 0, SX - 1), 1), pl.ds(jnp.clip(sy + j, 0, SY - 1), 1), :]
        return jnp.broadcast_to(row[0, :, k : k + 1], (8, 128))

    def half(pos, width):
        return jnp.where(pos < width, 0.5, 1.0).astype(F32)

    bands = {(i, j): (band(i, j, 0), band(i, j, 1)) for i in (-1, 0, 1) for j in (-1, 0, 1)}
    wrows = []
    for x in range(-R, NX + R):
        i = -1 if x < 0 else (1 if x >= NX else 0)
        row = half(jnp.full((8, 128), x - i * NX, jnp.int32), bands[i, 0][0]) * half(lane, bands[i, 0][1])
        cond = inside(i, 0)
        if cond is not None:
            row = row * jnp.where(cond, 1.0, 0.0).astype(F32)
        wrows.append(row)
    wpos = {0: lane // 6, -1: NX - R + (lane - 110) // 6, 1: (lane - 96) // 6}
    wstrips = []
    for i in (0, -1, 1):
        lane_i = (lane + 4) % 6 if i < 0 else lane6
        parts = []
        for j, pos in ((-1, NY - R + lane_i), (1, lane_i - R)):
            v = half(wpos[i], bands[i, j][0]) * half(pos, bands[i, j][1])
            parts.append(v * jnp.where(inside(i, j), 1.0, 0.0).astype(F32))
        wstrips.append(jnp.where(lane_i < R, parts[0], parts[1]))
    wstrips_at = (wstrips[0], jnp.where(lane < 110, wstrips[2], wstrips[1]), wstrips[2])

    total = psf[0]
    for j in range(1, 17):
        total = total + psf[j]

    row = lax.broadcasted_iota(jnp.int32, (256, 128), 0) % 128
    col = lax.broadcasted_iota(jnp.int32, (256, 128), 1)
    for n, pair in enumerate(PAIRS):
        for k, b in enumerate(pair):
            smat[n, :, 128 * k : 128 * k + 128] = jnp.where(row == col + (b - R), 1.0, 0.0).astype(BF16)
    lax.fori_loop(2, 10, make_taps, 0)

    def reciprocal(v):
        r = pltpu.reciprocal(v, approx=True)
        return r * (2.0 - v * r)

    def keep_norm(g, xs, values):
        sc = scr[rows8(g), :]
        acc = jnp.zeros((8, 128), F32)
        for x, v in zip(xs, values):
            r = reciprocal(v + spread_strip(sc, x))
            rnorm[x, rows8(g), :] = r
            acc = place(acc, r, x)
        pnorm[rows8(g), :] = acc

    def keep_lest(g, xs, values):
        for x, v in zip(xs, values):
            lest[x, rows8(g), :] = v

    def keep_update(g, xs, values):
        acc = pmain[rows8(g), :]
        for x, v in zip(xs, values):
            lest[x, rows8(g), :] = v
            acc = place(acc, v, x)
        pmain[rows8(g), :] = acc

    conv(rows_from(est1), False, INNER, 2, 10, 0, 2, 2, keep_lest)
    fwd1 = depth_matrix(48, 64, True)
    fwd2 = depth_matrix(32, 48, True)
    bwd = depth_matrix(64, 80, False)
    for c in tcopies:
        c.wait_recv()
    for g in (0, 1, 10, 11):
        make_taps(g, 0)

    def depth(part, spr, strip):
        blurs = []
        for a, b in part:
            pair = jnp.concatenate([lest[x] + spread_strip(scr[...], x) for x in (a, b)], axis=1)
            hi, lo = split3(pair)
            top = jnp.concatenate([hi[0:64], lo[0:64], hi[0:64]], axis=0)
            low = jnp.concatenate([hi[48:96], lo[48:96], hi[48:96]], axis=0)
            blurs.append(jnp.concatenate(
                [jnp.dot(fwd1, top, preferred_element_type=F32), jnp.dot(fwd2, low, preferred_element_type=F32)], axis=0))
        for (a, b), blur in zip(part, blurs):
            wide = jnp.concatenate([wrows[R + a][0:1], wrows[R + b][0:1]], axis=1)
            seen = jnp.concatenate([est1[R + a, 8:88, :], est1[R + b, 8:88, :]], axis=1)
            hi, lo = split3(wide * seen * reciprocal(blur))
            back = jnp.dot(bwd, jnp.concatenate([hi, lo, hi], axis=0), preferred_element_type=F32)
            for x, v in ((a, back[:, 0:128]), (b, back[:, 128:256])):
                spr[R + x] = v
                strip = [place(t, v[8 * g : 8 * g + 8], x) for g, t in enumerate(strip)]
        return strip

    for est, ye, qe, ecop, spr, ys, qs, scop, pks, last in (
        (est1, ye1, qe1, e1, spr1, ys1, qs1, s1, 1, False),
        (est2, ye2, qe2, e2, spr2, ys2, qs2, s2, 3, True),
    ):
        if last:
            conv(rows_from(est), False, INNER, 2, 10, 0, 2, 2, keep_lest)
        each(ecop, -1, "wait_recv", WAITS)
        unpack_corners(qe, HZ)
        halo_strips(*strips_from(ye), False, 0)
        conv(rows_from(est), False, EDGE, 0, EZ // 8, 0, 2, 6, keep_lest)
        strip = [jnp.zeros((8, 128), F32) for _ in range(NZ // 8)]
        strip = depth(((0, 1), (2, 13), (14, 15)), spr, strip)
        if last:
            each(s1, 1, "wait_send", WAITS)
        each(scop, 1, "start", X_FACE)
        pack_corners(strip, qk.at[pks])
        each(scop, 1, "start", CORN)
        conv(rows_from(est), False, INNER, 0, 2, 0, 2, 1, keep_lest)
        conv(rows_from(est), False, INNER, 10, 12, 0, 2, 1, keep_lest)
        strip = depth(((3, 4), (5, 6), (7, 8), (9, 10), (11, 12)), spr, strip)
        for g, t in enumerate(strip):
            pk[pks, 8 * g : 8 * g + 8, :] = t
        each(scop, 1, "start", Y_FACE)
        pmain[...] = jnp.zeros_like(pmain)
        conv(rows_from(spr), True, INNER, 0, NZ // 8, HZ, 2, 2, keep_update)
        if not last:
            halo_strips(*[jnp.concatenate([v] * (NZ // 8), axis=0) for v in wstrips_at], True, HZ)
            conv(lambda x, g: wrows[x], True, tuple(range(NX)), 0, NZ // 8, HZ, 1, 4, keep_norm)
        each(scop, -1, "wait_recv", WAITS)
        unpack_corners(qs, 0)
        halo_strips(*strips_from(ys), True, HZ)
        conv(rows_from(spr), True, EDGE, 0, NZ // 8, HZ, 2, 4, keep_update)

        def update(x):
            return est[R + x, HZ : HZ + NZ, :] * (lest[x, 0:NZ, :] + spread_strip(scr[0:NZ, :], x)) * rnorm[x]

        if last:
            for x in range(NX):
                res[x] = update(x)
        else:
            for x in EDGE:
                est2[R + x, HZ : HZ + NZ, :] = update(x)
            each(e1, 1, "wait_send", WAITS)
            each(e2, 1, "start", XS)
            pk[2] = pk[0] * (pmain[...] + scr[0:NZ, :]) * pnorm[...]
            pack_corners(packed_groups(2), qk.at[2])
            for x in INNER:
                est2[R + x, HZ : HZ + NZ, :] = update(x)
            each(e2, 1, "start", Z_FACE + CORN + SIDES)

    stores = [pltpu.make_async_copy(res.at[x], out.at[:, x, :], out_sem) for x in range(NX)]
    for c in stores:
        c.start()
    for c in tcopies:
        c.wait_send()
    for found in (e2, s2):
        each(found, 1, "wait_send", WAITS)
    pltpu.make_async_copy(res, res, out_sem).wait()


def body(observed, zone_of_slice, lateral_x, lateral_y, depth_psf, stitch_width):
    hbm = pl.BlockSpec(memory_space=pltpu.HBM)
    dma = pltpu.SemaphoreType.DMA
    return pl.pallas_call(
        kernel,
        out_shape=jax.ShapeDtypeStruct(observed.shape, F32),
        in_specs=[hbm] * 6,
        out_specs=hbm,
        scratch_shapes=[
            pltpu.SMEM((NZ,), jnp.int32), pltpu.VMEM((8, 7), F32), pltpu.VMEM((8, 7), F32),
            pltpu.SMEM((17,), F32), pltpu.VMEM((SX, SY, 2), jnp.int32), dma((5,)),
            pltpu.VMEM((EX, EZ, NY), F32), pltpu.VMEM((EX, EZ, NY), F32),
            pltpu.VMEM((EX, NZ, NY), F32), pltpu.VMEM((EX, NZ, NY), F32),
            pltpu.VMEM((4, NZ, 128), F32), pltpu.VMEM((4, 4, 8, 128), F32),
            pltpu.VMEM((2, EZ, 128), F32), pltpu.VMEM((2, EZ, 128), F32),
            pltpu.VMEM((2, NZ, 128), F32), pltpu.VMEM((2, NZ, 128), F32),
            pltpu.VMEM((2, 2, 3, 8, 128), F32), pltpu.VMEM((2, 2, 3, 8, 128), F32),
            pltpu.VMEM((2, 2, 3, 8, 128), F32), pltpu.VMEM((2, 2, 3, 8, 128), F32),
            pltpu.VMEM((2, EZ, 128), F32),
            pltpu.VMEM((NX, EZ, NY), F32), pltpu.VMEM((NX, NZ, NY), F32), pltpu.VMEM((NX, NZ, NY), F32),
            pltpu.VMEM((8, 128), F32), pltpu.VMEM((EZ, 128), F32), pltpu.VMEM((26, EZ, 128), F32),
            pltpu.VMEM((3, 256, 256), BF16), pltpu.VMEM((EZ, 128), F32),
            pltpu.VMEM((NZ, 128), F32), pltpu.VMEM((NZ, 128), F32),
            dma(()), dma(()), dma((2, 2)),
            dma((10,)), dma((10,)), dma((10,)), dma((8,)), dma((8,)), dma((8,)),
        ],
        compiler_params=pltpu.CompilerParams(collective_id=0, has_side_effects=True, vmem_limit_bytes=54500 * 1024),
        name="deconvolve",
    )(observed, zone_of_slice, lateral_x, lateral_y, depth_psf, stitch_width)


def solution(mesh):
    in_specs = (P("gz", "sx", "sy"), P("gz"), P(), P(), P(), P())
    out_specs = P("gz", "sx", "sy")
    return jax.shard_map(body, mesh=mesh, in_specs=in_specs, out_specs=out_specs, check_vma=False)
```

```python
import itertools
import jax
import jax.numpy as jnp
from jax import lax
from jax.experimental import pallas as pl
from jax.experimental.pallas import tpu as pltpu
from jax.sharding import PartitionSpec as P

MESH = pl.DeviceIdType.MESH
F32 = jnp.float32
BF16 = jnp.bfloat16
NX, NY, NZ = 16, 128, 64
R = 3
HZ = 16
EZ = NZ + 2 * HZ
EX = NX + 2 * R
SX, SY, GZ = 4, 4, 8
DIRS = [d for d in itertools.product((-1, 0, 1), repeat=3) if d != (0, 0, 0)]
SDIRS = [d for d in DIRS if d[2] == 0]
KX, KY, KF, KB = 0, 7, 14, 20
EDGE = (0, 1, 2, 13, 14, 15)
INNER = tuple(range(3, 13))
PAIRS = ((0, 1), (2, 4), (5, 6))
CORNERS = {(1, 1): (78, 110), (1, -1): (81, 113), (-1, 1): (0, 96), (-1, -1): (3, 99)}


def kernel(
    obs, zone_in, lat_x_in, lat_y_in, psf_in, stitch_in, out,
    zone, lat_x, lat_y, psf, stitch, small_sem,
    est1, est2, spr1, spr2, pk, qk, ye1, ye2, ys1, ys2, qe1, qe2, qs1, qs2, ch, lest, rnorm, res,
    ktab, taps, tb, smat, scr, pmain, pnorm, in_sem, out_sem, t_sem,
    es, er1, er2, ss, sr1, sr2,
):
    sx, sy, gz = lax.axis_index("sx"), lax.axis_index("sy"), lax.axis_index("gz")
    lane = lax.broadcasted_iota(jnp.int32, (8, 128), 1)
    lane6 = lane % 6
    edge = jnp.logical_or(lane < R, lane >= NY - R)
    lane_all = lax.broadcasted_iota(jnp.int32, (EZ, 128), 1)
    edge_all = jnp.logical_or(lane_all < R, lane_all >= NY - R)

    def rows8(g, off=0):
        if isinstance(g, int):
            return slice(g * 8 + off, g * 8 + off + 8)
        return pl.ds(pl.multiple_of(g * 8 + off, 8), 8)

    loads = [pltpu.make_async_copy(obs.at[:, x, :], est1.at[R + x, pl.ds(HZ, NZ)], in_sem) for x in range(NX)]
    smalls = [
        pltpu.make_async_copy(a, b, small_sem.at[i])
        for i, (a, b) in enumerate(((zone_in, zone), (lat_x_in, lat_x), (lat_y_in, lat_y), (psf_in, psf), (stitch_in, stitch)))
    ]
    for c in loads + smalls:
        c.start()

    def inside(dx, dy):
        ok = None
        for at, d, n in ((sx, dx, SX), (sy, dy, SY)):
            if d:
                t = at < n - 1 if d > 0 else at > 0
                ok = t if ok is None else jnp.logical_and(ok, t)
        return ok

    def guarded(cond, fn):
        if cond is None:
            fn()
        else:
            pl.when(cond)(fn)

    def device(dx, dy, dz):
        return (sx + dx, sy + dy, lax.rem(gz + dz + GZ, GZ))

    for dx, slot, rows in ((1, 0, 0), (-1, 1, EX - R)):
        @pl.when(jnp.logical_not(inside(-dx, 0)))
        def _(slot=slot, rows=rows):
            for e in (est1, est2, spr1, spr2):
                e[pl.ds(rows, R)] = jnp.zeros((R,) + e.shape[1:], F32)
            for q in (qe1, qe2, qs1, qs2):
                for side in range(2):
                    q[side, slot] = jnp.zeros(q.shape[2:], F32)
    for dy, side in ((1, 0), (-1, 1)):
        @pl.when(jnp.logical_not(inside(0, -dy)))
        def _(side=side):
            for y in (ye1, ye2, ys1, ys2, qe1, qe2, qs1, qs2):
                y[side] = jnp.zeros(y.shape[1:], F32)

    barrier = pltpu.get_barrier_semaphore()
    for dx, dy in itertools.product((-1, 0, 1), repeat=2):
        def greet(dx=dx, dy=dy):
            for dz in (-1, 0, 1):
                if (dx, dy, dz) != (0, 0, 0):
                    pl.semaphore_signal(barrier, inc=1, device_id=device(dx, dy, dz), device_id_type=MESH)
        guarded(inside(dx, dy), greet)

    def make_taps(g, _):
        rows = rows8(g)
        t = taps[rows, :]
        for i in range(14):
            tb[i, rows, :] = jnp.broadcast_to(t[:, i : i + 1], (8, 128))
        for k, b in enumerate((0, 1, 2, 4, 5, 6)):
            ok = {0: lane6 >= 3, 1: jnp.logical_or(lane6 == 3, lane6 == 4), 2: lane6 == 3,
                  4: lane6 == 2, 5: jnp.logical_or(lane6 == 1, lane6 == 2), 6: lane6 <= 2}[b]
            tb[KF + k, rows, :] = jnp.where(ok, jnp.broadcast_to(t[:, 7 + b : 8 + b], (8, 128)), 0.0)
            tb[KB + k, rows, :] = jnp.where(ok, jnp.broadcast_to(t[:, 13 - b : 14 - b], (8, 128)), 0.0)
        return 0


    def place(acc, v, x):
        at = jnp.logical_and(lane >= 6 * x, lane < 6 * x + 6)
        return jnp.where(at, pltpu.roll(v, 6 * x + R, 1), acc)

    def pack_block(src, off, dst):
        for g in range(NZ // 8):
            acc = jnp.zeros((8, 128), F32)
            for x in range(NX):
                acc = place(acc, src[R + x, g * 8 + off : g * 8 + off + 8, :], x)
            dst[g * 8 : g * 8 + 8, :] = acc

    def pack_corners(groups, dst):
        for k, (first, _) in enumerate(CORNERS.values()):
            acc = jnp.zeros((8, 128), F32)
            for g in range(NZ // 8):
                at = jnp.logical_and(lane >= 16 * g, lane < 16 * g + 16)
                acc = jnp.where(at, pltpu.roll(groups[g], (16 * g - first) % 128, 1), acc)
            dst[k] = acc

    def unpack_corners(src, halo):
        up = (lane + 4) % 6 < R
        for g in range((NZ + 2 * halo) // 8):
            slot, local = 1, g - halo // 8
            if local < 0:
                slot, local = 0, local + NZ // 8
            elif local >= NZ // 8:
                slot, local = 2, local - NZ // 8
            got = [pltpu.roll(src[0 if d[1] > 0 else 1, 0 if d[0] > 0 else 1, slot], (at - 16 * local) % 128, 1)
                   for d, (_, at) in CORNERS.items()]
            cu = jnp.where(up, got[0], got[1])
            cd = jnp.where(left, got[2], got[3])
            ch[0, g * 8 : g * 8 + 8, :] = jnp.where(lane < 110, cd, cu)
            ch[1, g * 8 : g * 8 + 8, :] = cd

    def place_of(dx, dy, dz):
        if (dx, dy) == (0, 0):
            return 8 if dz > 0 else 9
        return [d for d in itertools.product((-1, 0, 1), repeat=2) if d != (0, 0)].index((dx, dy))

    def copies(main, strips, packed, corners, cpacked, halo, dirs, send, recv):
        found = {}
        for dx, dy, dz in dirs:
            zs, zd, n = {0: (0, halo, NZ), 1: (NZ - HZ, 0, HZ), -1: (0, halo + NZ, HZ)}[dz]
            if dy == 0:
                xs, xd, m = {0: (R, R, NX), 1: (NX, 0, R), -1: (R, R + NX, R)}[dx]
                src = main.at[pl.ds(xs, m), pl.ds(halo + zs, n), :]
                dst = main.at[pl.ds(xd, m), pl.ds(zd, n), :]
            elif dx == 0:
                src = packed.at[pl.ds(zs, n), :]
                dst = strips.at[0 if dy > 0 else 1, pl.ds(zd, n), :]
            else:
                src = cpacked.at[list(CORNERS).index((dx, dy))]
                dst = corners.at[0 if dy > 0 else 1, 0 if dx > 0 else 1, 1 - dz]
            k = place_of(dx, dy, dz)
            found[(dx, dy, dz)] = pltpu.make_async_remote_copy(
                src_ref=src, dst_ref=dst, send_sem=send.at[k], recv_sem=recv.at[k],
                device_id=device(dx, dy, dz), device_id_type=MESH)
            if dz == 0:
                if dy == 0:
                    whole = main.at[pl.ds(xd, m)]
                elif dx == 0:
                    whole = strips.at[0 if dy > 0 else 1]
                elif halo:
                    whole = corners.at[0 if dy > 0 else 1, 0 if dx > 0 else 1]
                else:
                    whole = dst
                found[(dx, dy)] = pltpu.make_async_remote_copy(
                    src_ref=whole, dst_ref=whole, send_sem=send.at[k], recv_sem=recv.at[k],
                    device_id=device(dx, dy, 0), device_id_type=MESH)
        return found

    X_FACE, Z_FACE, Y_FACE = [(1, 0, 0), (-1, 0, 0)], [(0, 0, 1), (0, 0, -1)], [(0, 1, 0), (0, -1, 0)]
    XZ = [(dx, 0, dz) for dx in (1, -1) for dz in (1, -1)]
    YZ = [(0, dy, dz) for dy in (1, -1) for dz in (1, -1)]
    CORN = [(dx, dy, dz) for dx in (1, -1) for dy in (1, -1) for dz in (0, 1, -1)]
    XS = XZ + X_FACE
    WAITS = X_FACE + [d for d in CORN if d[2] == 0] + Y_FACE + Z_FACE
    SIDES = [(0, dy, dz) for dy in (1, -1) for dz in (1, -1, 0)]

    def each(found, sign, what, which):
        for (dx, dy), ds in itertools.groupby([d for d in which if d in found], key=lambda d: d[:2]):
            def go(ds=tuple(ds), dx=dx, dy=dy):
                if what != "start" and (dx, dy) in found:
                    ds = [(dx, dy)]
                for d in ds:
                    getattr(found[d], what)()
            guarded(inside(sign * dx, sign * dy), go)

    def taps_at(g, flip, off):
        trow = rows8(g, off)
        return ([tb[KX + (6 - a if flip else a), trow, :] for a in range(7)],
                [tb[KY + (6 - b if flip else b), trow, :] for b in range(7)])

    def halo_strips(c, c1, c2, flip, off):
        n = c.shape[0]
        rows = slice(off, off + n)
        own = lane_all[:n] < 96
        c1, c2 = jnp.where(own, c, c1), jnp.where(own, c, c2)
        al = tb[KX + 3, rows, :] * c
        for a in (0, 1, 2, 4, 5, 6):
            al = al + tb[KX + (6 - a if flip else a), rows, :] * pltpu.roll(c2 if a == 6 else c1, (18 - 6 * a) % 128, 1)
        sc = None
        for k, b in enumerate((0, 1, 2, 4, 5, 6)):
            v = tb[(KB if flip else KF) + k, rows, :] * pltpu.roll(al, (R - b) % 128, 1)
            sc = v if sc is None else sc + v
        scr[0:n, :] = sc

    def conv(rows_of, flip, xs, lo, hi, off, fuse, unroll, sink):
        def part(first):
            groups = [first + k for k in range(fuse)]
            along, taps_y = [], []
            for g in groups:
                kx, ky = taps_at(g, flip, off)
                taps_y.append(ky)
                rows = {}
                for x in xs:
                    for a in range(7):
                        if x + a not in rows:
                            rows[x + a] = rows_of(x + a, g)
                    v = kx[0] * rows[x]
                    for a in range(1, 7):
                        v = v + kx[a] * rows[x + a]
                    along.append(v)
            hi, lo_ = split3(jnp.concatenate(along, axis=0))
            both = jnp.concatenate([hi, lo_], axis=1)
            n = len(xs)
            acc = [taps_y[k // n][R] * v for k, v in enumerate(along)]
            for m, (b0, b1) in enumerate(PAIRS):
                moved = jnp.dot(both, smat[m], preferred_element_type=F32)
                for k in range(len(acc)):
                    ky = taps_y[k // n]
                    acc[k] = acc[k] + ky[b0] * moved[8 * k : 8 * k + 8, 0:128] + ky[b1] * moved[8 * k : 8 * k + 8, 128:256]
            for k, g in enumerate(groups):
                sink(g, xs, acc[k * n : k * n + n])

        def body(i, _):
            for k in range(unroll):
                part(lo + (i * unroll + k) * fuse)
            return 0

        if hi - lo == fuse * unroll:
            body(0, 0)
        else:
            lax.fori_loop(0, (hi - lo) // (fuse * unroll), body, 0)

    def spread_strip(v, x):
        return jnp.where(edge if v.shape[0] == 8 else edge_all[: v.shape[0]], pltpu.roll(v, (-(6 * x + R)) % 128, 1), 0.0)

    def rows_from(ref):
        return lambda x, g: ref[x, rows8(g), :]

    left = lane6 < R

    def strips_from(ref):
        n = ref.shape[1]
        return jnp.where(lane_all[:n] % 6 < R, ref[0], ref[1]), ch[0, 0:n, :], ch[1, 0:n, :]

    def depth_matrix(m, k, forward):
        off = lax.broadcasted_iota(jnp.int32, (m, k), 1) - lax.broadcasted_iota(jnp.int32, (m, k), 0)
        h = jnp.zeros((m, k), F32)
        for j in range(17):
            h = jnp.where(off == j, psf[16 - j if forward else j], h)
        h = h / jnp.full((m, k), total, F32)
        hi = h.astype(BF16)
        lo = (h - hi.astype(F32)).astype(BF16)
        return jnp.concatenate([hi, hi, lo], axis=1)

    def split3(v):
        hi = v.astype(BF16)
        lo = (v - hi.astype(F32)).astype(BF16)
        return hi, lo

    nx = 3 - (sx == 0).astype(jnp.int32) - (sx == SX - 1).astype(jnp.int32)
    ny = 3 - (sy == 0).astype(jnp.int32) - (sy == SY - 1).astype(jnp.int32)
    for c in smalls:
        c.wait()
    mine = est1.at[pl.ds(R, NX), pl.ds(HZ, NZ)]
    pltpu.make_async_copy(mine, mine, in_sem).wait()
    pl.semaphore_wait(barrier, nx * ny * 3 - 1)

    tcopies = [
        pltpu.make_async_remote_copy(
            src_ref=taps.at[pl.ds(s, HZ), :], dst_ref=taps.at[pl.ds(d, HZ), :],
            send_sem=t_sem.at[0, i], recv_sem=t_sem.at[1, i], device_id=device(0, 0, dz), device_id_type=MESH)
        for i, (dz, s, d) in enumerate(((1, NZ, 0), (-1, HZ, HZ + NZ)))
    ]
    e1 = copies(est1, ye1, pk.at[0], qe1, qk.at[0], HZ, DIRS, es, er1)
    s1 = copies(spr1, ys1, pk.at[1], qs1, qk.at[1], 0, SDIRS, ss, sr1)
    e2 = copies(est2, ye2, pk.at[2], qe2, qk.at[2], HZ, DIRS, es, er2)
    s2 = copies(spr2, ys2, pk.at[3], qs2, qk.at[3], 0, SDIRS, ss, sr2)

    def packed_groups(k):
        return [pk[k, 8 * g : 8 * g + 8, :] for g in range(NZ // 8)]

    each(e1, 1, "start", XS + Z_FACE)
    pack_block(est1, HZ, pk.at[0])
    pack_corners(packed_groups(0), qk.at[0])
    each(e1, 1, "start", CORN + SIDES)

    ktab[...] = jnp.zeros((8, 128), F32)
    ktab[:, 0:7] = lat_x[...]
    ktab[:, 7:14] = lat_y[...]
    for z in range(NZ):
        taps[HZ + z : HZ + z + 1, :] = ktab[pl.ds(zone[z], 1), :]
    for c in tcopies:
        c.start()

    def band(i, j, k):
        row = stitch[pl.ds(jnp.clip(sx + i, 0, SX - 1), 1), pl.ds(jnp.clip(sy + j, 0, SY - 1), 1), :]
        return jnp.broadcast_to(row[0, :, k : k + 1], (8, 128))

    def half(pos, width):
        return jnp.where(pos < width, 0.5, 1.0).astype(F32)

    bands = {(i, j): (band(i, j, 0), band(i, j, 1)) for i in (-1, 0, 1) for j in (-1, 0, 1)}
    wrows = []
    for x in range(-R, NX + R):
        i = -1 if x < 0 else (1 if x >= NX else 0)
        row = half(jnp.full((8, 128), x - i * NX, jnp.int32), bands[i, 0][0]) * half(lane, bands[i, 0][1])
        cond = inside(i, 0)
        if cond is not None:
            row = row * jnp.where(cond, 1.0, 0.0).astype(F32)
        wrows.append(row)
    wpos = {0: lane // 6, -1: NX - R + (lane - 110) // 6, 1: (lane - 96) // 6}
    wstrips = []
    for i in (0, -1, 1):
        lane_i = (lane + 4) % 6 if i < 0 else lane6
        parts = []
        for j, pos in ((-1, NY - R + lane_i), (1, lane_i - R)):
            v = half(wpos[i], bands[i, j][0]) * half(pos, bands[i, j][1])
            parts.append(v * jnp.where(inside(i, j), 1.0, 0.0).astype(F32))
        wstrips.append(jnp.where(lane_i < R, parts[0], parts[1]))
    wstrips_at = (wstrips[0], jnp.where(lane < 110, wstrips[2], wstrips[1]), wstrips[2])

    total = psf[0]
    for j in range(1, 17):
        total = total + psf[j]

    row = lax.broadcasted_iota(jnp.int32, (256, 128), 0) % 128
    col = lax.broadcasted_iota(jnp.int32, (256, 128), 1)
    for n, pair in enumerate(PAIRS):
        for k, b in enumerate(pair):
            smat[n, :, 128 * k : 128 * k + 128] = jnp.where(row == col + (b - R), 1.0, 0.0).astype(BF16)
    lax.fori_loop(2, 10, make_taps, 0)

    def reciprocal(v):
        r = pltpu.reciprocal(v, approx=True)
        return r * (2.0 - v * r)

    def keep_norm(g, xs, values):
        sc = scr[rows8(g), :]
        acc = jnp.zeros((8, 128), F32)
        for x, v in zip(xs, values):
            r = reciprocal(v + spread_strip(sc, x))
            rnorm[x, rows8(g), :] = r
            acc = place(acc, r, x)
        pnorm[rows8(g), :] = acc

    def keep_lest(g, xs, values):
        for x, v in zip(xs, values):
            lest[x, rows8(g), :] = v

    def keep_update(g, xs, values):
        acc = pmain[rows8(g), :]
        for x, v in zip(xs, values):
            lest[x, rows8(g), :] = v
            acc = place(acc, v, x)
        pmain[rows8(g), :] = acc

    conv(rows_from(est1), False, INNER, 2, 10, 0, 2, 2, keep_lest)
    fwd1 = depth_matrix(48, 64, True)
    fwd2 = depth_matrix(32, 48, True)
    bwd = depth_matrix(64, 80, False)
    for c in tcopies:
        c.wait_recv()
    for g in (0, 1, 10, 11):
        make_taps(g, 0)

    def depth(part, spr, strip):
        blurs = []
        for a, b in part:
            pair = jnp.concatenate([lest[x] + spread_strip(scr[...], x) for x in (a, b)], axis=1)
            hi, lo = split3(pair)
            top = jnp.concatenate([hi[0:64], lo[0:64], hi[0:64]], axis=0)
            low = jnp.concatenate([hi[48:96], lo[48:96], hi[48:96]], axis=0)
            blurs.append(jnp.concatenate(
                [jnp.dot(fwd1, top, preferred_element_type=F32), jnp.dot(fwd2, low, preferred_element_type=F32)], axis=0))
        for (a, b), blur in zip(part, blurs):
            wide = jnp.concatenate([wrows[R + a][0:1], wrows[R + b][0:1]], axis=1)
            seen = jnp.concatenate([est1[R + a, 8:88, :], est1[R + b, 8:88, :]], axis=1)
            hi, lo = split3(wide * seen * reciprocal(blur))
            back = jnp.dot(bwd, jnp.concatenate([hi, lo, hi], axis=0), preferred_element_type=F32)
            for x, v in ((a, back[:, 0:128]), (b, back[:, 128:256])):
                spr[R + x] = v
                strip = [place(t, v[8 * g : 8 * g + 8], x) for g, t in enumerate(strip)]
        return strip

    for est, ye, qe, ecop, spr, ys, qs, scop, pks, last in (
        (est1, ye1, qe1, e1, spr1, ys1, qs1, s1, 1, False),
        (est2, ye2, qe2, e2, spr2, ys2, qs2, s2, 3, True),
    ):
        if last:
            conv(rows_from(est), False, INNER, 2, 10, 0, 2, 2, keep_lest)
        each(ecop, -1, "wait_recv", WAITS)
        unpack_corners(qe, HZ)
        halo_strips(*strips_from(ye), False, 0)
        conv(rows_from(est), False, EDGE, 0, EZ // 8, 0, 2, 6, keep_lest)
        strip = [jnp.zeros((8, 128), F32) for _ in range(NZ // 8)]
        strip = depth(((0, 1), (2, 13), (14, 15)), spr, strip)
        if last:
            each(s1, 1, "wait_send", WAITS)
        pack_corners(strip, qk.at[pks])
        each(scop, 1, "start", CORN + X_FACE)
        conv(rows_from(est), False, INNER, 0, 2, 0, 2, 1, keep_lest)
        conv(rows_from(est), False, INNER, 10, 12, 0, 2, 1, keep_lest)
        strip = depth(((3, 4), (5, 6), (7, 8), (9, 10), (11, 12)), spr, strip)
        for g, t in enumerate(strip):
            pk[pks, 8 * g : 8 * g + 8, :] = t
        each(scop, 1, "start", Y_FACE)
        pmain[...] = jnp.zeros_like(pmain)
        conv(rows_from(spr), True, INNER, 0, NZ // 8, HZ, 2, 2, keep_update)
        if not last:
            halo_strips(*[jnp.concatenate([v] * (NZ // 8), axis=0) for v in wstrips_at], True, HZ)
            conv(lambda x, g: wrows[x], True, tuple(range(NX)), 0, NZ // 8, HZ, 1, 4, keep_norm)
        each(scop, -1, "wait_recv", WAITS)
        unpack_corners(qs, 0)
        halo_strips(*strips_from(ys), True, HZ)
        conv(rows_from(spr), True, EDGE, 0, NZ // 8, HZ, 2, 4, keep_update)

        def update(x):
            return est[R + x, HZ : HZ + NZ, :] * (lest[x, 0:NZ, :] + spread_strip(scr[0:NZ, :], x)) * rnorm[x]

        if last:
            for x in range(NX):
                res[x] = update(x)
        else:
            for x in EDGE:
                est2[R + x, HZ : HZ + NZ, :] = update(x)
            each(e1, 1, "wait_send", WAITS)
            each(e2, 1, "start", XS)
            pk[2] = pk[0] * (pmain[...] + scr[0:NZ, :]) * pnorm[...]
            pack_corners(packed_groups(2), qk.at[2])
            for x in INNER:
                est2[R + x, HZ : HZ + NZ, :] = update(x)
            each(e2, 1, "start", CORN + SIDES + Z_FACE)

    stores = [pltpu.make_async_copy(res.at[x], out.at[:, x, :], out_sem) for x in range(NX)]
    for c in stores:
        c.start()
    for c in tcopies:
        c.wait_send()
    for found in (e2, s2):
        each(found, 1, "wait_send", WAITS)
    pltpu.make_async_copy(res, res, out_sem).wait()


def body(observed, zone_of_slice, lateral_x, lateral_y, depth_psf, stitch_width):
    hbm = pl.BlockSpec(memory_space=pltpu.HBM)
    dma = pltpu.SemaphoreType.DMA
    return pl.pallas_call(
        kernel,
        out_shape=jax.ShapeDtypeStruct(observed.shape, F32),
        in_specs=[hbm] * 6,
        out_specs=hbm,
        scratch_shapes=[
            pltpu.SMEM((NZ,), jnp.int32), pltpu.VMEM((8, 7), F32), pltpu.VMEM((8, 7), F32),
            pltpu.SMEM((17,), F32), pltpu.VMEM((SX, SY, 2), jnp.int32), dma((5,)),
            pltpu.VMEM((EX, EZ, NY), F32), pltpu.VMEM((EX, EZ, NY), F32),
            pltpu.VMEM((EX, NZ, NY), F32), pltpu.VMEM((EX, NZ, NY), F32),
            pltpu.VMEM((4, NZ, 128), F32), pltpu.VMEM((4, 4, 8, 128), F32),
            pltpu.VMEM((2, EZ, 128), F32), pltpu.VMEM((2, EZ, 128), F32),
            pltpu.VMEM((2, NZ, 128), F32), pltpu.VMEM((2, NZ, 128), F32),
            pltpu.VMEM((2, 2, 3, 8, 128), F32), pltpu.VMEM((2, 2, 3, 8, 128), F32),
            pltpu.VMEM((2, 2, 3, 8, 128), F32), pltpu.VMEM((2, 2, 3, 8, 128), F32),
            pltpu.VMEM((2, EZ, 128), F32),
            pltpu.VMEM((NX, EZ, NY), F32), pltpu.VMEM((NX, NZ, NY), F32), pltpu.VMEM((NX, NZ, NY), F32),
            pltpu.VMEM((8, 128), F32), pltpu.VMEM((EZ, 128), F32), pltpu.VMEM((26, EZ, 128), F32),
            pltpu.VMEM((3, 256, 256), BF16), pltpu.VMEM((EZ, 128), F32),
            pltpu.VMEM((NZ, 128), F32), pltpu.VMEM((NZ, 128), F32),
            dma(()), dma(()), dma((2, 2)),
            dma((10,)), dma((10,)), dma((10,)), dma((8,)), dma((8,)), dma((8,)),
        ],
        compiler_params=pltpu.CompilerParams(collective_id=0, has_side_effects=True, vmem_limit_bytes=54500 * 1024),
        name="deconvolve",
    )(observed, zone_of_slice, lateral_x, lateral_y, depth_psf, stitch_width)


def solution(mesh):
    in_specs = (P("gz", "sx", "sy"), P("gz"), P(), P(), P(), P())
    out_specs = P("gz", "sx", "sy")
    return jax.shard_map(body, mesh=mesh, in_specs=in_specs, out_specs=out_specs, check_vma=False)
```
